512 devices in a mesh: kv: 32 (over z, core), mp: 16 (over y, x).
Axes of the slice: x: 4, y: 4, z: 16, core: 2. Of those that a mesh axis runs over, the one named last changes fastest.
Arguments:
- queries: bfloat16 [32, 8192], P(None, ('kv', 'mp')), may hold values from -200 to 200
- key_value_pages: bfloat16 [1024, 128, 8, 256], P('kv', 'mp'), may hold values from -12 to 12
- request_page_index: int32 [32, 32], replicated, may hold values from -1 to 1023, as said below
- lengths: int32 [32], replicated, may hold values from 1024 to 4096, as said below
- request_adapter_index: int32 [32], replicated, may hold values from 0 to 63
- output_weight: bfloat16 [8192, 8192], P('mp', 'kv'), may hold values from -0.5 to 0.5
- down_weight_columns: bfloat16 [8192, 1024], P('mp'), may hold values from -0.5 to 0.5
- up_weight_rows: bfloat16 [1024, 8192], P(None, 'kv'), may hold values from -0.75 to 0.75
Outputs:
- block_output: bfloat16 [32, 8192], P('mp', 'kv')
The draws below stay inside these ranges and needn't reach their ends.
Inputs may be any that keep to these rules, and one draw needn't show every extreme that they name: `request_page_index`: row r holds the pages of request r in order: its first ceil(lengths[r] / 128) entries are pages of 0 to 1023, no page in two places, the others -1. Page p lies on index p // 32 of kv. `lengths`: some request has exactly 4096.
All inputs are finite; a program needn't handle non-finite values.
Results may differ from the reference program's by a relative error of at most 0.017.
Values may be sent and summed in bfloat16 or wider, within the bound.
No kernel may reach another device: no remote copies, remote signals or barrier semaphores. Data moves between devices by JAX's collectives and lax.ppermute only.
A program may use at most 64 MiB of HBM per device.

```python
import math
import jax
import jax.numpy as jnp
from jax import lax

MODEL_WIDTH = 8192
QUERY_HEADS = 64
KV_HEADS = 8
HEAD_WIDTH = 128
PAGE = 128
MAXP = 32
ADAPTER_COUNT = 64
ADAPTER_RANK = 16
REQUEST_COUNT = 32
POOL_DEV = 32
POOL = 1024


def page_plan(key):
    base = jax.random.fold_in(key, 202)
    first, second, third, fourth = jax.random.split(base, 4)
    longest = MAXP * PAGE
    drawn = jax.random.randint(first, (REQUEST_COUNT,), longest // 4, longest + 1)
    chosen = jax.random.randint(second, (), 0, REQUEST_COUNT)
    lengths = jnp.where(jnp.arange(REQUEST_COUNT) == chosen, longest, drawn).astype(jnp.int32)
    counts = (lengths + PAGE - 1) // PAGE
    holders = POOL // POOL_DEV
    favour = jax.random.randint(third, (holders,), 0, 3)
    noise = jax.random.randint(fourth, (POOL,), 0, 1024)
    page_ids = jnp.arange(POOL, dtype=jnp.int32)
    ranking = (favour[page_ids // POOL_DEV] * 1024 + noise) * POOL + page_ids
    order = jnp.argsort(-ranking, stable=True).astype(jnp.int32)
    offsets = jnp.cumsum(counts) - counts
    slots = jnp.arange(MAXP, dtype=jnp.int32)
    index = jnp.minimum(offsets[:, None] + slots[None, :], POOL - 1)
    table = jnp.where(slots[None, :] < counts[:, None], order[index], -1).astype(jnp.int32)
    return (lengths, table)


def draw_request_page_index(key, part):
    lengths, table = page_plan(key)
    return table


def draw_lengths(key, part):
    lengths, table = page_plan(key)
    return lengths


def draw_queries(key, part):
    key = jax.random.fold_in(key, 1)
    group = QUERY_HEADS // KV_HEADS
    second = jax.random.fold_in(key, 1)
    values = jnp.clip(2.0 * jax.random.normal(second, (REQUEST_COUNT, KV_HEADS, group, HEAD_WIDTH), jnp.float32), -8.0, 8.0)
    return values.reshape(REQUEST_COUNT, QUERY_HEADS * HEAD_WIDTH).astype(jnp.bfloat16)


def draw_key_value_pages(key, part):
    key = jax.random.fold_in(key, 2)
    second = jax.random.fold_in(key, 1)
    third = jax.random.fold_in(key, 2)
    keys = jnp.clip(jax.random.normal(second, (POOL, PAGE, KV_HEADS, HEAD_WIDTH), jnp.float32), -6.0, 6.0)
    values = jnp.clip(jax.random.normal(third, (POOL, PAGE, KV_HEADS, HEAD_WIDTH), jnp.float32), -6.0, 6.0)
    return jnp.concatenate([keys, values], axis=-1).astype(jnp.bfloat16)


def place_ends(entries, key, least, top_value):
    extent = entries.shape
    index_at = [jax.random.randint(jax.random.fold_in(key, axis), (), 0, extent[axis]) for axis in range(len(extent))]
    entries = entries.at[tuple(index_at)].set(least)
    longest = extent.index(max(extent))
    index_at[longest] = (index_at[longest] + 1) % extent[longest]
    return entries.at[tuple(index_at)].set(top_value)


def shard_levels(own_key, dims, cuts, smallest, high):
    def one(dim, blocks):
        heights = jax.random.uniform(jax.random.fold_in(jax.random.fold_in(own_key, 6), dim), (blocks,), jnp.float32, smallest / len(cuts), high / len(cuts))
        return jnp.repeat(jnp.exp(heights), dims[dim] // blocks).reshape((-1,) + (1,) * (len(dims) - dim - 1))

    level = one(*cuts[0])
    for cut in cuts[1:]:
        level = level * one(*cut)
    return level


def scatter_about(stream_key, extent, scale, limit, shards=(), kind=jnp.bfloat16):
    values = jax.random.normal(stream_key, extent, jnp.float32) * scale
    if len(shards) > 0:
        values = shard_levels(stream_key, extent, shards, -0.22, 0.18) * values
    return jnp.clip(values, min=-limit, max=limit).astype(kind)


def setup_inputs(seed: int = 0) -> dict:
    key_of = jax.random.split(jax.random.key(seed), 9)
    queries = draw_queries(jax.random.fold_in(key_of[8], 71), 0)
    key_value_pages = draw_key_value_pages(jax.random.fold_in(key_of[8], 71), 0)
    request_page_index = draw_request_page_index(jax.random.fold_in(key_of[8], 71), 0)
    lengths = draw_lengths(jax.random.fold_in(key_of[8], 71), 0)
    request_adapter_index = place_ends(jax.random.randint(key_of[4], (REQUEST_COUNT,), 0, ADAPTER_COUNT), jax.random.fold_in(key_of[4], 1), 0, ADAPTER_COUNT - 1).astype(jnp.int32)
    output_weight = scatter_about(key_of[5], (QUERY_HEADS * HEAD_WIDTH, MODEL_WIDTH), (QUERY_HEADS * HEAD_WIDTH // 64) ** -0.5, 0.5, ((0, 16), (1, 32)))
    down_weight_columns = scatter_about(key_of[6], (QUERY_HEADS * HEAD_WIDTH, ADAPTER_COUNT * ADAPTER_RANK), (QUERY_HEADS * HEAD_WIDTH // 64) ** -0.5, 0.5, ((0, 16),))
    up_weight_rows = scatter_about(key_of[7], (ADAPTER_COUNT * ADAPTER_RANK, MODEL_WIDTH), (ADAPTER_RANK * 4) ** -0.5, 0.75, ((1, 32),))
    return {"queries": queries, "key_value_pages": key_value_pages, "request_page_index": request_page_index, "lengths": lengths, "request_adapter_index": request_adapter_index, "output_weight": output_weight, "down_weight_columns": down_weight_columns, "up_weight_rows": up_weight_rows}


NEG = -1e+30
ADAPTER_SCALE = 2.0

def reference(queries, key_value_pages, request_page_index, lengths, request_adapter_index, output_weight, down_weight_columns, up_weight_rows):
    group = QUERY_HEADS // KV_HEADS
    span = MAXP * PAGE
    scale = 1.0 / math.sqrt(HEAD_WIDTH)

    def attend_request(items):
        query_row, pages, length = items
        cached = key_value_pages[jnp.maximum(pages, 0)].reshape(span, KV_HEADS, 2 * HEAD_WIDTH)
        keys_f = cached[:, :, :HEAD_WIDTH].astype(jnp.float32)
        values_f = cached[:, :, HEAD_WIDTH:].astype(jnp.float32)
        query_f = query_row.reshape(KV_HEADS, group, HEAD_WIDTH).astype(jnp.float32)
        scores = jnp.einsum('kgd,tkd->kgt', query_f, keys_f) * scale
        valid = jnp.arange(span) < length
        scores = jnp.where(valid, scores, NEG)
        top = lax.optimization_barrier(jnp.max(scores, axis=-1, keepdims=True))
        weights = jnp.where(valid, jnp.exp(scores - top), 0.0)
        total = lax.optimization_barrier(jnp.sum(weights, axis=-1))
        rounded = lax.optimization_barrier(weights.astype(jnp.bfloat16)).astype(jnp.float32)
        mixed = jnp.einsum('kgt,tkd->kgd', rounded, values_f) / total[..., None]
        return mixed.reshape(QUERY_HEADS * HEAD_WIDTH).astype(jnp.bfloat16)
    attention_output = lax.map(attend_request, (queries, request_page_index, lengths))
    projected_output = jnp.dot(attention_output, output_weight, preferred_element_type=jnp.float32)
    rank_reduced = jnp.dot(attention_output, down_weight_columns, preferred_element_type=jnp.float32).reshape(REQUEST_COUNT, ADAPTER_COUNT, ADAPTER_RANK)
    select = (request_adapter_index[:, None] == jnp.arange(ADAPTER_COUNT, dtype=jnp.int32)[None, :]).astype(jnp.float32)
    rank_terms = lax.optimization_barrier(jnp.sum(rank_reduced * select[:, :, None], axis=1))
    expanded_update = (select[:, :, None] * rank_terms[:, None, :]).reshape(REQUEST_COUNT, ADAPTER_COUNT * ADAPTER_RANK)
    adapter_update = ADAPTER_SCALE * jnp.dot(expanded_update, up_weight_rows.astype(jnp.float32), precision=lax.Precision.HIGHEST)
    return (projected_output + adapter_update).astype(jnp.bfloat16)
```

```python
import math

import jax
import jax.numpy as jnp
import numpy as np
from jax import lax
from jax.experimental import pallas as pl
from jax.experimental.pallas import tpu as pltpu
from jax.sharding import Mesh
from jax.sharding import PartitionSpec as P

RANK = 16
LOW = -1e30
FLOOR = -1e20
ADAPTER_SCALE = 2.0

KV = ("zh", "zl", "c")
MP = ("y", "xh", "xl")
NEAR = ("zl", "c")
SPLIT = ("zl", "c", "xl")

bf16 = jnp.bfloat16
f32 = jnp.float32


def exchange(value, axes):
    return lax.all_to_all(value, axes, split_axis=0, concat_axis=0, tiled=True)


def call(kernel, out_shape, *operands, scratch=(), vmem=None):
    return pl.pallas_call(
        kernel,
        out_shape=out_shape,
        in_specs=[pl.BlockSpec(memory_space=pltpu.VMEM)] * len(operands),
        out_specs=pl.BlockSpec(memory_space=pltpu.VMEM),
        scratch_shapes=list(scratch),
        compiler_params=pltpu.CompilerParams(vmem_limit_bytes=vmem or 16 * 1024 * 1024),
    )(*operands)


def pack_queries(q_ref, out_ref):
    q = q_ref[...].astype(f32)
    requests, width = q.shape
    lanes = 4 * requests
    row = lax.broadcasted_iota(jnp.int32, (requests, lanes), 0)
    lane = lax.broadcasted_iota(jnp.int32, (requests, lanes), 1)
    packed = jnp.zeros((4, lanes), f32)
    for u in range(4):
        place = (lane == row + u * requests).astype(f32)
        packed = packed + lax.dot_general(
            q[:, 4 * u : 4 * u + 4],
            place,
            (((0,), (0,)), ((), ())),
            preferred_element_type=f32,
        )
    out_ref[...] = jnp.broadcast_to(packed.astype(bf16)[None], out_ref.shape)


def regroup_queries(x_ref, out_ref):
    x = x_ref[...].astype(f32).reshape(8, 4, 4, 128)
    group = lax.broadcasted_iota(jnp.int32, (32, 128), 1) // 32
    blocks = [x[:, i].reshape(32, 128) for i in range(4)]
    rows = []
    for u in range(4):
        merged = jnp.zeros((32, 128), f32)
        for i in range(4):
            moved = pltpu.roll(blocks[i], (32 * (i - u)) % 128, 1) if i != u else blocks[i]
            merged = jnp.where(group == i, moved, merged)
        rows.append(merged.reshape(8, 1, 4, 128))
    whole = jnp.concatenate(rows, axis=1).reshape(8, 16, 128).astype(bf16)
    out_ref[...] = jnp.broadcast_to(whole[:, None], (8, 2, 16, 128)).reshape(16, 16, 128)


def attend(scale, q_ref, kv_ref, count_ref, out_ref, s_ref):
    queries = jnp.concatenate(
        [q_ref[0:8].reshape(128, 128), q_ref[8:16].reshape(128, 128)], axis=1
    )
    parts = kv_ref.shape[0]
    token = lax.broadcasted_iota(jnp.int32, (16, 8, 128), 1)
    room = (count_ref[...][:, None, :] - token).reshape(128, 128)
    room = jnp.concatenate([room, room], axis=1)
    peak = jnp.full((1, 256), FLOOR, f32)
    for j in range(parts):
        scores = jnp.dot(kv_ref[j, :, :128], queries, preferred_element_type=f32) * scale
        scores = jnp.where(room > 8 * j, scores, LOW)
        s_ref[j] = scores
        peak = jnp.maximum(peak, jnp.max(scores, axis=0, keepdims=True))
    total = jnp.zeros((1, 256), f32)
    mixed = jnp.zeros((128, 256), f32)
    for j in range(parts):
        weights = jnp.exp(s_ref[j] - peak)
        total = total + jnp.sum(weights, axis=0, keepdims=True)
        mixed = mixed + lax.dot_general(
            kv_ref[j, :, 128:],
            weights.astype(bf16),
            (((0,), (0,)), ((), ())),
            preferred_element_type=f32,
        )
    outputs = mixed.T
    pair = jnp.concatenate(
        [jnp.broadcast_to(peak, (64, 256)), jnp.broadcast_to(total, (64, 256))], axis=0
    ).T
    for bit0 in range(2):
        for half in range(2):
            for bit1 in range(2):
                for c in range(2):
                    start = ((bit0 * 2 + half) * 2 + bit1) * 32 + 16 * c
                    to = ((bit0 * 2 + bit1) * 2 + c) * 2 + half
                    out_ref[to, 0:16, :] = outputs[start : start + 16]
                    out_ref[to, 16:32, :] = pair[start : start + 16]


def merged(x_ref):
    outputs = x_ref[:, 0:16, :]
    pair = x_ref[:, 16:32, :]
    peaks = pair[:, :, 0:1]
    totals = pair[:, :, 64:65]
    peak = jnp.max(peaks, axis=0)
    factor = jnp.exp(peaks - peak[None])
    total = jnp.sum(factor * totals, axis=0)
    return jnp.sum(factor * outputs, axis=0), peak, total


def merge_near(x_ref, out_ref):
    outputs, peak, total = merged(x_ref)
    lane = lax.broadcasted_iota(jnp.int32, (16, 128), 1)
    pair = jnp.where(lane < 64, peak, total)
    for k in range(out_ref.shape[0]):
        out_ref[k, 0:16, :] = outputs
        out_ref[k, 16:32, :] = pair


def merge_far(x_ref, out_ref):
    outputs, _, total = merged(x_ref)
    attended = (outputs / total).astype(bf16)
    out_ref[...] = jnp.broadcast_to(attended[None], out_ref.shape)


def project(att_ref, adapter_ref, weight_ref, down_ref, up_ref, out_ref):
    att = att_ref[...].reshape(4, 32, 128)
    projected = jnp.zeros((32, 256), f32)
    reduced = jnp.zeros((32, down_ref.shape[1]), f32)
    for part, head in enumerate((0, 2, 1, 3)):
        rows = slice(128 * head, 128 * head + 128)
        projected = projected + jnp.dot(
            att[part], weight_ref[rows, :], preferred_element_type=f32
        )
        reduced = reduced + jnp.dot(att[part], down_ref[rows, :], preferred_element_type=f32)
    column = lax.broadcasted_iota(jnp.int32, reduced.shape, 1)
    chosen = jnp.where(column // RANK == adapter_ref[...], reduced, 0.0)
    upper = chosen.astype(bf16)
    lower = (chosen - upper.astype(f32)).astype(bf16)
    both = jnp.dot(
        jnp.concatenate([upper, lower], axis=0), up_ref[...], preferred_element_type=f32
    )
    result = projected + ADAPTER_SCALE * (both[:32] + both[32:])
    for j in range(16):
        out_ref[j, 0:2, :] = result[2 * j : 2 * j + 2, :128]
        out_ref[j, 2:4, :] = result[2 * j : 2 * j + 2, 128:]


def finish(x_ref, out_ref):
    result = jnp.sum(x_ref[...], axis=0)
    out_ref[:, 0:128] = result[0:2].astype(out_ref.dtype)
    out_ref[:, 128:256] = result[2:4].astype(out_ref.dtype)


def on_device(
    queries,
    key_value_pages,
    request_page_index,
    lengths,
    request_adapter_index,
    output_weight,
    down_weight_columns,
    up_weight_rows,
):
    shape = jax.ShapeDtypeStruct
    requests = lengths.shape[0]
    pages_here, slice_tokens, kv_heads, row = key_value_pages.shape
    page_size = slice_tokens * lax.axis_size(MP)
    scale = 1.0 / math.sqrt(row // 2)

    with jax.named_scope("queries_over_kv"):
        packed = call(pack_queries, shape((32, 4, 128), bf16), queries)
        spread = exchange(packed, KV)
    with jax.named_scope("pages_by_head"):
        half = pages_here // 2
        by_head = key_value_pages.reshape(2, half * slice_tokens, kv_heads, row)
        by_head = by_head.transpose(2, 0, 1, 3).reshape(16, half * slice_tokens, row)
        pages = exchange(by_head, MP)
    with jax.named_scope("counts"):
        first = lax.axis_index(KV) * pages_here + lax.axis_index("xl") * half
        ids = first + jnp.arange(half, dtype=jnp.int32)
        starts = page_size * jnp.arange(request_page_index.shape[1], dtype=jnp.int32)
        inside = jnp.clip(lengths[:, None] - starts[None, :], 0, page_size)
        match = request_page_index[None] == ids[:, None, None]
        count = jnp.sum(jnp.where(match, inside[None], 0), axis=2)
        count = jnp.tile(count, (1, 128 // requests))
    with jax.named_scope("queries_over_mp"):
        regrouped = call(regroup_queries, shape((16, 16, 128), bf16), spread)
        own_queries = exchange(regrouped, MP)
    with jax.named_scope("attention"):
        partial = call(
            lambda *refs: attend(scale, *refs),
            shape((16, 32, 128), f32),
            own_queries,
            pages,
            count,
            scratch=[pltpu.VMEM((16, 128, 256), f32)],
        )
    with jax.named_scope("merge"):
        near = call(merge_near, shape((4, 32, 128), f32), exchange(partial, SPLIT))
        attended = call(merge_far, shape((8, 16, 128), bf16), exchange(near, ("zh",)))
        attended = exchange(attended, NEAR)
    with jax.named_scope("projection"):
        result = call(
            project,
            shape((16, 4, 128), f32),
            attended,
            request_adapter_index[:, None],
            output_weight,
            down_weight_columns,
            up_weight_rows,
        )
        return call(finish, shape((2, 256), bf16), exchange(result, MP))


def solution(mesh):
    fine = Mesh(mesh.devices.reshape(4, 4, 2, 4, 2, 2), KV + MP)
    in_specs = (
        P(None, KV + MP),
        P(KV, MP, None, None),
        P(),
        P(),
        P(),
        P(MP, KV),
        P(MP, None),
        P(None, KV),
    )
    return jax.shard_map(
        on_device, mesh=fine, in_specs=in_specs, out_specs=P(MP, KV), check_vma=False
    )
```

```python
import math

import jax
import jax.numpy as jnp
import numpy as np
from jax import lax
from jax.experimental import pallas as pl
from jax.experimental.pallas import tpu as pltpu
from jax.sharding import Mesh
from jax.sharding import PartitionSpec as P

RANK = 16
LOW = -1e30
FLOOR = -1e20
ADAPTER_SCALE = 2.0

KV = ("zo", "zn", "c")
MP = ("y", "xh", "xl")
NEAR = ("zn", "c")
SPLIT = ("zn", "c", "xl")
FAR = ("zo",)

bf16 = jnp.bfloat16
f32 = jnp.float32


def exchange(value, axes):
    return lax.all_to_all(value, axes, split_axis=0, concat_axis=0, tiled=True)


def call(kernel, out_shape, *operands, scratch=(), vmem=None):
    return pl.pallas_call(
        kernel,
        out_shape=out_shape,
        in_specs=[pl.BlockSpec(memory_space=pltpu.VMEM)] * len(operands),
        out_specs=pl.BlockSpec(memory_space=pltpu.VMEM),
        scratch_shapes=list(scratch),
        compiler_params=pltpu.CompilerParams(vmem_limit_bytes=vmem or 16 * 1024 * 1024),
    )(*operands)


def pack_queries(q_ref, out_ref):
    q = q_ref[...].astype(f32)
    requests = q.shape[1]
    row = lax.broadcasted_iota(jnp.int32, (requests, 128), 0)
    lane = lax.broadcasted_iota(jnp.int32, (requests, 128), 1)
    packed = jnp.zeros((4, 128), f32)
    for u in range(4):
        place = (lane == row + u * requests).astype(f32)
        packed = packed + jnp.dot(q[4 * u : 4 * u + 4], place, preferred_element_type=f32)
    out_ref[...] = jnp.broadcast_to(packed.astype(bf16)[None], out_ref.shape)


def regroup_queries(x_ref, out_ref):
    x = x_ref[...].astype(f32).reshape(8, 4, 4, 128)
    group = lax.broadcasted_iota(jnp.int32, (32, 128), 1) // 32
    blocks = [x[:, i].reshape(32, 128) for i in range(4)]
    rows = []
    for u in range(4):
        merged = jnp.zeros((32, 128), f32)
        for i in range(4):
            moved = pltpu.roll(blocks[i], (32 * (i - u)) % 128, 1) if i != u else blocks[i]
            merged = jnp.where(group == i, moved, merged)
        rows.append(merged.reshape(8, 1, 4, 128))
    whole = jnp.concatenate(rows, axis=1).reshape(8, 16, 128).astype(bf16)
    out_ref[...] = jnp.broadcast_to(whole[:, None], (8, 2, 16, 128)).reshape(16, 16, 128)


def attend(scale, x_ref, count_ref, out_ref, s_ref):
    queries = x_ref[:, 256:272, :]
    queries = jnp.concatenate(
        [queries[0:8].reshape(128, 128), queries[8:16].reshape(128, 128)], axis=1
    )
    parts = x_ref.shape[0]
    token = lax.broadcasted_iota(jnp.int32, (16, 8, 128), 1)
    room = (count_ref[...][:, None, :] - token).reshape(128, 128)
    room = jnp.concatenate([room, room], axis=1)
    peak = jnp.full((1, 256), FLOOR, f32)
    for j in range(parts):
        scores = jnp.dot(x_ref[j, 0:128, :], queries, preferred_element_type=f32) * scale
        scores = jnp.where(room > 8 * j, scores, LOW)
        s_ref[j] = scores
        peak = jnp.maximum(peak, jnp.max(scores, axis=0, keepdims=True))
    total = jnp.zeros((1, 256), f32)
    mixed = jnp.zeros((128, 256), f32)
    for j in range(parts):
        weights = jnp.exp(s_ref[j] - peak)
        total = total + jnp.sum(weights, axis=0, keepdims=True)
        mixed = mixed + lax.dot_general(
            x_ref[j, 128:256, :],
            weights.astype(bf16),
            (((0,), (0,)), ((), ())),
            preferred_element_type=f32,
        )
    outputs = mixed.T
    row = lax.broadcasted_iota(jnp.int32, (128, 256), 0)
    pair = jnp.where(row % 32 < 16, peak, total).T
    lane = lax.broadcasted_iota(jnp.int32, (8, 128), 1)
    for bit0 in range(2):
        for half in range(2):
            for bit1 in range(2):
                start = ((bit0 * 2 + half) * 2 + bit1) * 32
                to = (bit0 * 2 + bit1) * 2 + half
                out_ref[to, 0:32, :] = outputs[start : start + 32]
                packed = pair[start : start + 8]
                for block in range(1, 4):
                    rows = pair[start + 8 * block : start + 8 * block + 8]
                    packed = jnp.where(lane // 32 == block, rows, packed)
                out_ref[to, 32:40, :] = packed


def merge(outputs, peaks, totals):
    peak = jnp.max(peaks, axis=0)
    factor = jnp.exp(peaks - peak[None])
    return jnp.sum(factor * outputs, axis=0), peak, jnp.sum(factor * totals, axis=0)


def thirds(value):
    parts = []
    for _ in range(3):
        parts.append(value.astype(bf16).astype(f32))
        value = value - parts[-1]
    return parts


def merge_near(x_ref, out_ref):
    blocks = []
    for block in range(4):
        lane = 32 * block
        blocks.append(
            merge(
                x_ref[:, 8 * block : 8 * block + 8, :],
                x_ref[:, 32:40, lane : lane + 1],
                x_ref[:, 32:40, lane + 16 : lane + 17],
            )
        )
    outputs, peak, total = (jnp.concatenate(part, axis=0) for part in zip(*blocks))
    columns = []
    for rows in (slice(0, 16), slice(16, 32)):
        columns += thirds(peak[rows]) + thirds(total[rows])
    lane = lax.broadcasted_iota(jnp.int32, (16, 128), 1)
    tile = jnp.zeros((16, 128), f32)
    for place, column in enumerate(columns):
        tile = jnp.where(lane // 8 == place, column, tile)
    whole = jnp.concatenate([outputs, tile], axis=0).astype(bf16)
    out_ref[...] = jnp.broadcast_to(whole[None], out_ref.shape)


def merge_far(x_ref, out_ref):
    tile = x_ref[:, 32:48, :].astype(f32)

    def column(place):
        parts = [
            sum(tile[:, :, 8 * (first + k) : 8 * (first + k) + 1] for k in range(3))
            for first in (place, place + 6)
        ]
        return jnp.concatenate(parts, axis=1)

    outputs, _, total = merge(x_ref[:, 0:32, :].astype(f32), column(0), column(3))
    attended = (outputs * (1.0 / total)).astype(bf16)
    out_ref[...] = jnp.broadcast_to(attended[None], out_ref.shape)


def project(att_ref, adapter_ref, weight_ref, down_ref, up_ref, out_ref):
    att = att_ref[...]
    projected = jnp.zeros((32, 256), f32)
    reduced = jnp.zeros((32, down_ref.shape[1]), f32)
    for part, head in enumerate((0, 2, 1, 3)):
        rows = slice(128 * head, 128 * head + 128)
        projected = projected + jnp.dot(
            att[part], weight_ref[rows, :], preferred_element_type=f32
        )
        reduced = reduced + jnp.dot(att[part], down_ref[rows, :], preferred_element_type=f32)
    column = lax.broadcasted_iota(jnp.int32, reduced.shape, 1)
    chosen = jnp.where(column // RANK == adapter_ref[...], reduced, 0.0)
    upper = chosen.astype(bf16)
    lower = (chosen - upper.astype(f32)).astype(bf16)
    both = jnp.dot(
        jnp.concatenate([upper, lower], axis=0), up_ref[...], preferred_element_type=f32
    )
    result = projected + ADAPTER_SCALE * (both[:32] + both[32:])
    for j in range(16):
        out_ref[j, 0:2, :] = result[2 * j : 2 * j + 2, :128]
        out_ref[j, 2:4, :] = result[2 * j : 2 * j + 2, 128:]


def finish(x_ref, out_ref):
    result = jnp.sum(x_ref[...], axis=0)
    out_ref[:, 0:128] = result[0:2].astype(out_ref.dtype)
    out_ref[:, 128:256] = result[2:4].astype(out_ref.dtype)


def on_device(
    queries,
    key_value_pages,
    request_page_index,
    lengths,
    request_adapter_index,
    output_weight,
    down_weight_columns,
    up_weight_rows,
):
    shape = jax.ShapeDtypeStruct
    requests = lengths.shape[0]
    pages_here, slice_tokens, kv_heads, row = key_value_pages.shape
    page_size = slice_tokens * lax.axis_size(MP)
    scale = 1.0 / math.sqrt(row // 2)

    half = pages_here // 2
    with jax.named_scope("queries_over_kv"):
        packed = call(pack_queries, shape((32, 4, 128), bf16), queries.T)
        spread = exchange(packed, KV)
    with jax.named_scope("pages_by_head"):
        tokens = half * slice_tokens
        by_head = key_value_pages.reshape(2, tokens, kv_heads, 2, row // 2)
        by_head = by_head.transpose(2, 0, 3, 1, 4).reshape(16, 2 * tokens, row // 2)
        by_head = jnp.pad(by_head, ((0, 0), (0, 16), (0, 0)))
    with jax.named_scope("counts"):
        first = lax.axis_index(KV) * pages_here + lax.axis_index("xl") * half
        ids = first + jnp.arange(half, dtype=jnp.int32)
        starts = page_size * jnp.arange(request_page_index.shape[1], dtype=jnp.int32)
        inside = jnp.clip(lengths[:, None] - starts[None, :], 0, page_size)
        match = request_page_index[None] == ids[:, None, None]
        count = jnp.sum(jnp.where(match, inside[None], 0), axis=2)
        count = jnp.tile(count, (1, 128 // requests))
    with jax.named_scope("queries_and_pages_over_mp"):
        spread, by_head, count = lax.optimization_barrier((spread, by_head, count))
        regrouped = call(regroup_queries, shape((16, 16, 128), bf16), spread)
        sent = lax.dynamic_update_slice(by_head, regrouped, (0, 2 * tokens, 0))
        arrived = exchange(sent, MP)
    with jax.named_scope("attention"):
        partial = call(
            lambda *refs: attend(scale, *refs),
            shape((8, 40, 128), f32),
            arrived,
            count,
            scratch=[pltpu.VMEM((16, 128, 256), f32)],
        )
    with jax.named_scope("merge"):
        near = call(merge_near, shape((8, 48, 128), bf16), exchange(partial, SPLIT))
        attended = call(merge_far, shape((4, 32, 128), bf16), exchange(near, FAR))
        attended = exchange(attended, NEAR)
    with jax.named_scope("projection"):
        result = call(
            project,
            shape((16, 4, 128), f32),
            attended,
            request_adapter_index[:, None],
            output_weight,
            down_weight_columns,
            up_weight_rows,
        )
        return call(finish, shape((2, 256), bf16), exchange(result, MP))


def solution(mesh):
    fine = Mesh(mesh.devices.reshape(8, 2, 2, 4, 2, 2), KV + MP)
    in_specs = (
        P(None, KV + MP),
        P(KV, MP, None, None),
        P(),
        P(),
        P(),
        P(MP, KV),
        P(MP, None),
        P(None, KV),
    )
    return jax.shard_map(
        on_device, mesh=fine, in_specs=in_specs, out_specs=P(MP, KV), check_vma=False
    )
```

```python
import math

import jax
import jax.numpy as jnp
from jax import lax
from jax.experimental import pallas as pl
from jax.experimental.pallas import tpu as pltpu
from jax.sharding import Mesh
from jax.sharding import PartitionSpec as P

RANK = 16
LOW = -1e30
FLOOR = -1e20
ADAPTER_SCALE = 2.0

KV = ("zo", "zn", "c")
MP = ("y", "x")
NEAR = ("zn", "c")
SPLIT = ("zn", "c", "x")
FAR = ("zo",)

bf16 = jnp.bfloat16
f32 = jnp.float32
i32 = jnp.int32


QUERY_FIRST = 24
MERGE_FIRST = 3


def exchange(value, axes, first=0):
    members = value.shape[0]
    groups = [[(first + k) % members for k in range(members)]] if first else None
    return lax.all_to_all(
        value, axes, split_axis=0, concat_axis=0, tiled=True, axis_index_groups=groups
    )


def call(kernel, out_shape, *operands, scratch=(), cost=None):
    return pl.pallas_call(
        kernel,
        out_shape=out_shape,
        in_specs=[pl.BlockSpec(memory_space=pltpu.VMEM)] * len(operands),
        out_specs=jax.tree.map(lambda _: pl.BlockSpec(memory_space=pltpu.VMEM), out_shape),
        scratch_shapes=list(scratch),
        cost_estimate=cost,
        compiler_params=pltpu.CompilerParams(vmem_limit_bytes=16 * 1024 * 1024),
    )(*operands)


def prepare(page_size, *refs):
    given, outs, held, scratch = refs[0:5], refs[5:12], refs[12:16], refs[16:]
    out_ref, count_ref, own_ref, *piece_refs = outs
    kv_ref, wide_ref, packed_ref, sems = scratch
    loads = [
        pltpu.make_async_copy(from_ref, to_ref, sems.at[k])
        for k, (from_ref, to_ref) in enumerate(zip(given, held))
    ]
    parts = 4
    pages = kv_ref.shape[0] // parts
    kv_loads = [
        pltpu.make_async_copy(
            given[4].at[pl.ds(pages * k, pages)], kv_ref.at[pl.ds(pages * k, pages)], sems.at[4 + k]
        )
        for k in range(parts)
    ]
    for load in loads + kv_loads:
        load.start()
    q_ref, table_ref, length_ref, adapter_ref = held
    loads[0].wait()
    q = q_ref[...].astype(f32)
    requests = q.shape[1]
    row = lax.broadcasted_iota(i32, (requests, 128), 0)
    lane = lax.broadcasted_iota(i32, (requests, 128), 1)
    packed = jnp.zeros((4, 128), f32)
    for u in range(4):
        place = (lane == row + u * requests).astype(f32)
        packed = packed + jnp.dot(q[4 * u : 4 * u + 4], place, preferred_element_type=f32)
    packed_ref[...] = jnp.broadcast_to(packed.astype(bf16)[None], packed_ref.shape)
    store = pltpu.make_async_copy(packed_ref, out_ref, sems.at[8])
    store.start()
    tokens = pages * kv_ref.shape[1]
    y = lax.axis_index("y")
    for k, load in enumerate(kv_loads):
        load.wait()
        wide = kv_ref[pages * k : pages * k + pages].astype(f32).reshape(8 * tokens, 256)
        wide_ref[0] = wide[:, :128]
        wide_ref[1] = wide[:, 128:]
        for step, piece_ref in enumerate(piece_refs):
            for head in range(2):
                first = 2 * lax.rem(y + step, 4) + head
                for side in range(2):
                    rows = wide_ref[side, pl.ds(first, tokens, stride=8), :]
                    to = slice(tokens * k, tokens * k + tokens)
                    piece_ref[head, side, to, :] = rows.astype(bf16)
    for load in loads[1:]:
        load.wait()
    pages = count_ref.shape[0]
    first = lax.axis_index(KV) * pages
    table = jnp.concatenate([table_ref[...]] * 4, axis=0).astype(f32)
    table = jnp.concatenate([table] * 4, axis=1).T[: table_ref.shape[1]].astype(i32)
    length = jnp.concatenate([length_ref[...]] * 4, axis=1)
    start = page_size * lax.broadcasted_iota(i32, table.shape, 0)
    inside = jnp.clip(length - start, 0, page_size).astype(f32)
    for page in range(pages):
        found = jnp.where(table == first + page, inside, 0.0)
        count_ref[page : page + 1, :] = jnp.sum(found, axis=0, keepdims=True)
    adapter = jnp.concatenate([adapter_ref[...]] * 4, axis=1).astype(f32)
    adapter = jnp.sum(jnp.where(lane == row, adapter, 0.0), axis=1, keepdims=True)
    own_ref[...] = jnp.broadcast_to(adapter, own_ref.shape).astype(i32)
    store.wait()


def regroup_queries(x_ref, out_ref):
    x = x_ref[...].astype(f32)
    x = jnp.concatenate([x[32 - QUERY_FIRST :], x[: 32 - QUERY_FIRST]], axis=0)
    x = x.reshape(8, 4, 4, 128)
    group = lax.broadcasted_iota(i32, (32, 128), 1) // 32
    blocks = [x[:, i].reshape(32, 128) for i in range(4)]
    rows = []
    for u in range(4):
        merged = jnp.zeros((32, 128), f32)
        for i in range(4):
            moved = pltpu.roll(blocks[i], (32 * (i - u)) % 128, 1) if i != u else blocks[i]
            merged = jnp.where(group == i, moved, merged)
        rows.append(merged.reshape(8, 1, 4, 128))
    whole = jnp.concatenate(rows, axis=1).reshape(4, 1, 2, 16, 128).astype(bf16)
    out_ref[...] = jnp.broadcast_to(whole, (4, 4, 2, 16, 128)).reshape(16, 2, 16, 128)


def thirds(value):
    parts = []
    for _ in range(3):
        parts.append(value.astype(bf16).astype(f32))
        value = value - parts[-1]
    return parts


def encode(outputs, peak, total):
    columns = []
    for rows in (slice(0, 16), slice(16, 32)):
        columns += thirds(peak[rows]) + thirds(total[rows])
    lane = lax.broadcasted_iota(i32, (16, 128), 1)
    tile = jnp.zeros((16, 128), f32)
    for place, column in enumerate(columns):
        tile = jnp.where(lane // 8 == place, column, tile)
    return jnp.concatenate([outputs, tile], axis=0).astype(bf16)


def merged(x_ref):
    tile = x_ref[:, 32:48, :].astype(f32)

    def column(place):
        parts = [
            sum(tile[:, :, 8 * (first + k) : 8 * (first + k) + 1] for k in range(3))
            for first in (place, place + 6)
        ]
        return jnp.concatenate(parts, axis=1)

    peaks, totals = column(0), column(3)
    peak = jnp.max(peaks, axis=0)
    factor = jnp.exp(peaks - peak[None])
    outputs = jnp.sum(factor * x_ref[:, 0:32, :].astype(f32), axis=0)
    return outputs, peak, jnp.sum(factor * totals, axis=0)


def merge_near(x_ref, out_ref):
    out_ref[...] = jnp.broadcast_to(encode(*merged(x_ref))[None], out_ref.shape)


def merge_far(x_ref, out_ref):
    outputs, _, total = merged(x_ref)
    attended = (outputs * (1.0 / total)).astype(bf16)
    out_ref[...] = jnp.broadcast_to(attended[None], out_ref.shape)


def attend(scale, q_ref, own_ref, *refs):
    *piece_refs, count_ref, out_ref, s_ref = refs
    y, x = lax.axis_index("y"), lax.axis_index("x")
    pages = count_ref.shape[0]
    tokens = 8 * pages
    token = lax.broadcasted_iota(i32, (pages, 8, 128), 1)
    room = (count_ref[...].astype(i32)[:, None, :] - token).reshape(tokens, 128)
    room = jnp.concatenate([room, room], axis=1)
    pieces = [own_ref] + list(piece_refs)
    places = [8 * (4 * lax.rem(y + 4 - step, 4) + x) for step in range(4)]
    for head in range(2):
        queries = q_ref[:, head]
        queries = jnp.concatenate(
            [queries[0:8].reshape(128, 128), queries[8:16].reshape(128, 128)], axis=1
        )
        peak = jnp.full((1, 256), FLOOR, f32)
        for step in range(4):
            scores = jnp.dot(pieces[step][head, 0], queries, preferred_element_type=f32)
            scores = jnp.where(room > places[step], scores * scale, LOW)
            s_ref[step] = scores
            peak = jnp.maximum(peak, jnp.max(scores, axis=0, keepdims=True))
        total = jnp.zeros((1, 256), f32)
        mixed = jnp.zeros((128, 256), f32)
        for step in range(4):
            weights = jnp.exp(s_ref[step] - peak)
            total = total + jnp.sum(weights, axis=0, keepdims=True)
            mixed = mixed + lax.dot_general(
                pieces[step][head, 1],
                weights.astype(bf16),
                (((0,), (0,)), ((), ())),
                preferred_element_type=f32,
            )
        outputs = mixed.T
        row = lax.broadcasted_iota(i32, (128, 256), 0)
        pair = jnp.where(row < 64, peak, total).T
        for bit0 in range(2):
            for half in range(2):
                for bit1 in range(2):
                    start = ((bit0 * 2 + half) * 2 + bit1) * 32
                    rows = slice(start, start + 32)
                    to = (bit0 * 2 + bit1) * 4 + head * 2 + half
                    out_ref[to] = encode(outputs[rows], pair[rows, 0:1], pair[rows, 64:65])


def project(att_ref, adapter_ref, weight_ref, down_ref, up_ref, out_ref, rows_ref):
    projected = jnp.zeros((32, 256), f32)
    reduced = jnp.zeros((32, down_ref.shape[1]), f32)
    for part, head in enumerate((0, 2, 1, 3)):
        rows = slice(128 * head, 128 * head + 128)
        projected = projected + jnp.dot(
            att_ref[part], weight_ref[rows, :], preferred_element_type=f32
        )
        reduced = reduced + jnp.dot(att_ref[part], down_ref[rows, :], preferred_element_type=f32)
    column = lax.broadcasted_iota(i32, reduced.shape, 1)
    chosen = jnp.where(column // RANK == adapter_ref[:, 0:1], reduced, 0.0)
    upper = chosen.astype(bf16)
    lower = (chosen - upper.astype(f32)).astype(bf16)
    both = jnp.dot(
        jnp.concatenate([upper, lower], axis=0), up_ref[...], preferred_element_type=f32
    )
    result = projected + ADAPTER_SCALE * (both[:32] + both[32:])
    for j in range(16):
        rows_ref[j, 0:2, :] = result[2 * j : 2 * j + 2, :128]
        rows_ref[j, 2:4, :] = result[2 * j : 2 * j + 2, 128:]
    out_ref[...] = rows_ref[...].astype(bf16)


def finish(x_ref, out_ref):
    result = jnp.sum(x_ref[...].astype(f32), axis=0)
    out_ref[:, 0:128] = result[0:2].astype(out_ref.dtype)
    out_ref[:, 128:256] = result[2:4].astype(out_ref.dtype)


def on_device(
    queries,
    key_value_pages,
    request_page_index,
    lengths,
    request_adapter_index,
    output_weight,
    down_weight_columns,
    up_weight_rows,
):
    shape = jax.ShapeDtypeStruct
    pages_here, slice_tokens, kv_heads, row = key_value_pages.shape
    page_size = slice_tokens * lax.axis_size(MP)
    scale = 1.0 / math.sqrt(row // 2)

    with jax.named_scope("queries_over_kv"):
        tokens = pages_here * slice_tokens
        given = (
            queries.T,
            request_page_index,
            lengths[None],
            request_adapter_index[None],
            key_value_pages,
        )
        anywhere = pl.BlockSpec(memory_space=pl.ANY)
        local = pl.BlockSpec(memory_space=pltpu.VMEM)
        packed, count, adapter, own, *pieces = pl.pallas_call(
            lambda *refs: prepare(page_size, *refs),
            out_shape=(
                shape((32, 4, 128), bf16),
                shape((pages_here, 128), f32),
                shape((32, 128), i32),
            )
            + (shape((2, 2, tokens, row // 2), bf16),) * 4,
            in_specs=[anywhere] * 5,
            out_specs=(anywhere,) + (local,) * 6,
            scratch_shapes=[pltpu.VMEM(part.shape, part.dtype) for part in given]
            + [
                pltpu.VMEM((2, tokens // 4 * kv_heads, row // 2), f32),
                pltpu.VMEM((32, 4, 128), bf16),
                pltpu.SemaphoreType.DMA((9,)),
            ],
        )(*given)
        spread = exchange(packed, KV, QUERY_FIRST)
    with jax.named_scope("pages_over_y"):
        for step in range(1, 4):
            ring = [(k, (k + step) % 4) for k in range(4)]
            pieces[step - 1] = lax.ppermute(pieces[step - 1], "y", ring)
    with jax.named_scope("queries_over_mp"):
        regrouped = call(
            regroup_queries,
            shape((16, 2, 16, 128), bf16),
            spread,
            cost=pl.CostEstimate(flops=10**11, bytes_accessed=10**8, transcendentals=0),
        )
        own_queries = exchange(regrouped, MP)
    with jax.named_scope("attention"):
        partial = call(
            lambda *refs: attend(scale, *refs),
            shape((16, 48, 128), bf16),
            own_queries,
            own,
            *pieces,
            count,
            scratch=[pltpu.VMEM((4, 256, 256), f32)],
        )
    with jax.named_scope("merge"):
        near = call(merge_near, shape((8, 48, 128), bf16), exchange(partial, SPLIT))
        attended = call(merge_far, shape((4, 32, 128), bf16), exchange(near, FAR, MERGE_FIRST))
        attended = exchange(attended, NEAR)
    with jax.named_scope("projection"):
        result = call(
            project,
            shape((16, 4, 128), bf16),
            attended,
            adapter,
            output_weight,
            down_weight_columns,
            up_weight_rows,
            scratch=[pltpu.VMEM((16, 4, 128), f32)],
        )
        return call(finish, shape((2, 256), bf16), exchange(result, MP))


def solution(mesh):
    fine = Mesh(mesh.devices.reshape(8, 2, 2, 4, 4), KV + MP)
    in_specs = (
        P(None, KV + MP),
        P(KV, MP, None, None),
        P(),
        P(),
        P(),
        P(MP, KV),
        P(MP, None),
        P(None, KV),
    )
    return jax.shard_map(
        on_device, mesh=fine, in_specs=in_specs, out_specs=P(MP, KV), check_vma=False
    )
```

```python
import math

import jax
import jax.numpy as jnp
from jax import lax
from jax.experimental import pallas as pl
from jax.experimental.pallas import tpu as pltpu
from jax.sharding import Mesh
from jax.sharding import PartitionSpec as P

RANK = 16
LOW = -1e30
FLOOR = -1e20
ADAPTER_SCALE = 2.0

KV = ("zo", "zn", "c")
MP = ("y", "x")
NEAR = ("zn", "c")
SPLIT = ("zn", "c", "x")
FAR = ("zo",)

bf16 = jnp.bfloat16
f32 = jnp.float32
i32 = jnp.int32


QUERY_FIRST = 24
MERGE_FIRST = 3


def exchange(value, axes, first=0):
    members = value.shape[0]
    groups = [[(first + k) % members for k in range(members)]] if first else None
    return lax.all_to_all(
        value, axes, split_axis=0, concat_axis=0, tiled=True, axis_index_groups=groups
    )


def call(kernel, out_shape, *operands, scratch=(), cost=None):
    return pl.pallas_call(
        kernel,
        out_shape=out_shape,
        in_specs=[pl.BlockSpec(memory_space=pltpu.VMEM)] * len(operands),
        out_specs=jax.tree.map(lambda _: pl.BlockSpec(memory_space=pltpu.VMEM), out_shape),
        scratch_shapes=list(scratch),
        cost_estimate=cost,
        compiler_params=pltpu.CompilerParams(vmem_limit_bytes=16 * 1024 * 1024),
    )(*operands)


def pack_queries(q_ref, out_ref):
    q = q_ref[...].astype(f32)
    requests = q.shape[1]
    row = lax.broadcasted_iota(i32, (requests, 128), 0)
    lane = lax.broadcasted_iota(i32, (requests, 128), 1)
    packed = jnp.zeros((4, 128), f32)
    for u in range(4):
        place = (lane == row + u * requests).astype(f32)
        packed = packed + jnp.dot(q[4 * u : 4 * u + 4], place, preferred_element_type=f32)
    out_ref[...] = jnp.broadcast_to(packed.astype(bf16)[None], out_ref.shape)


def sort_pages(kv_ref, *refs):
    *piece_refs, wide_ref = refs
    parts = 4
    pages = kv_ref.shape[0] // parts
    tokens = pages * kv_ref.shape[1]
    y = lax.axis_index("y")
    for k in range(parts):
        wide = kv_ref[pages * k : pages * k + pages].astype(f32).reshape(8 * tokens, 256)
        wide_ref[0] = wide[:, :128]
        wide_ref[1] = wide[:, 128:]
        for step, piece_ref in enumerate(piece_refs):
            for head in range(2):
                first = 2 * lax.rem(y + step, 4) + head
                for side in range(2):
                    rows = wide_ref[side, pl.ds(first, tokens, stride=8), :]
                    to = slice(tokens * k, tokens * k + tokens)
                    piece_ref[head, side, to, :] = rows.astype(bf16)


def count_tokens(page_size, pages, table_ref, length_ref):
    first = lax.axis_index(KV) * pages
    table = jnp.concatenate([table_ref[...]] * 4, axis=0).astype(f32)
    table = jnp.concatenate([table] * 4, axis=1).T[: table_ref.shape[1]].astype(i32)
    length = jnp.concatenate([length_ref[...].reshape(1, 32)] * 4, axis=1)
    start = page_size * lax.broadcasted_iota(i32, table.shape, 0)
    inside = jnp.clip(length - start, 0, page_size).astype(f32)
    rows = [
        jnp.sum(jnp.where(table == first + page, inside, 0.0), axis=0, keepdims=True)
        for page in range(pages)
    ]
    return jnp.concatenate(rows, axis=0).astype(i32)


def regroup_queries(x_ref, out_ref):
    x = x_ref[...].astype(f32)
    x = jnp.concatenate([x[32 - QUERY_FIRST :], x[: 32 - QUERY_FIRST]], axis=0)
    x = x.reshape(8, 4, 4, 128)
    group = lax.broadcasted_iota(i32, (32, 128), 1) // 32
    blocks = [x[:, i].reshape(32, 128) for i in range(4)]
    rows = []
    for u in range(4):
        merged = jnp.zeros((32, 128), f32)
        for i in range(4):
            moved = pltpu.roll(blocks[i], (32 * (i - u)) % 128, 1) if i != u else blocks[i]
            merged = jnp.where(group == i, moved, merged)
        rows.append(merged.reshape(8, 1, 4, 128))
    whole = jnp.concatenate(rows, axis=1).reshape(4, 1, 2, 16, 128).astype(bf16)
    out_ref[...] = jnp.broadcast_to(whole, (4, 4, 2, 16, 128)).reshape(16, 2, 16, 128)


def thirds(value):
    parts = []
    for _ in range(3):
        parts.append(value.astype(bf16).astype(f32))
        value = value - parts[-1]
    return parts


def encode(outputs, peak, total):
    columns = []
    for block in range(4):
        rows = slice(8 * block, 8 * block + 8)
        columns += thirds(peak[rows]) + thirds(total[rows])
    lane = lax.broadcasted_iota(i32, (8, 128), 1)
    tile = jnp.zeros((8, 128), f32)
    for place, column in enumerate(columns):
        tile = jnp.where(lane // 5 == place, column, tile)
    return jnp.concatenate([outputs, tile], axis=0).astype(bf16)


def merged(x_ref):
    x = x_ref[...].astype(f32)
    tile = x[:, 32:40]

    def column(place):
        parts = [
            sum(tile[:, :, 5 * (first + k) : 5 * (first + k) + 1] for k in range(3))
            for first in range(place, 24, 6)
        ]
        return jnp.concatenate(parts, axis=1)

    peaks, totals = column(0), column(3)
    peak = jnp.max(peaks, axis=0)
    factor = jnp.exp(peaks - peak[None])
    outputs = jnp.sum(factor * x[:, 0:32], axis=0)
    return outputs, peak, jnp.sum(factor * totals, axis=0)


def merge_near(x_ref, out_ref):
    out_ref[...] = jnp.broadcast_to(encode(*merged(x_ref))[None], out_ref.shape)


def merge_far(x_ref, out_ref):
    outputs, _, total = merged(x_ref)
    attended = (outputs * (1.0 / total)).astype(bf16)
    out_ref[...] = jnp.broadcast_to(attended[None], out_ref.shape)


def attend(scale, page_size, q_ref, *refs):
    *pieces, table_ref, length_ref, adapter_ref, out_ref, own_ref, s_ref = refs
    y, x = lax.axis_index("y"), lax.axis_index("x")
    tokens = pieces[0].shape[2]
    pages = tokens // 8
    count = count_tokens(page_size, pages, table_ref, length_ref)
    token = lax.broadcasted_iota(i32, (pages, 8, 128), 1)
    room = (count[:, None, :] - token).reshape(tokens, 128)
    room = jnp.concatenate([room, room], axis=1)
    places = [8 * (4 * lax.rem(y + 4 - step, 4) + x) for step in range(4)]
    for head in range(2):
        queries = q_ref[:, head]
        queries = jnp.concatenate(
            [queries[0:8].reshape(128, 128), queries[8:16].reshape(128, 128)], axis=1
        )
        peak = jnp.full((1, 256), FLOOR, f32)
        for step in range(4):
            scores = jnp.dot(pieces[step][head, 0], queries, preferred_element_type=f32)
            scores = jnp.where(room > places[step], scores * scale, LOW)
            s_ref[step] = scores
            peak = jnp.maximum(peak, jnp.max(scores, axis=0, keepdims=True))
        total = jnp.zeros((1, 256), f32)
        mixed = jnp.zeros((128, 256), f32)
        for step in range(4):
            weights = jnp.exp(s_ref[step] - peak)
            total = total + jnp.sum(weights, axis=0, keepdims=True)
            mixed = mixed + lax.dot_general(
                pieces[step][head, 1],
                weights.astype(bf16),
                (((0,), (0,)), ((), ())),
                preferred_element_type=f32,
            )
        outputs = mixed.T
        row = lax.broadcasted_iota(i32, (128, 256), 0)
        pair = jnp.where(row < 64, peak, total).T
        for bit0 in range(2):
            for half in range(2):
                for bit1 in range(2):
                    start = ((bit0 * 2 + half) * 2 + bit1) * 32
                    rows = slice(start, start + 32)
                    to = (bit0 * 2 + bit1) * 4 + head * 2 + half
                    out_ref[to] = encode(outputs[rows], pair[rows, 0:1], pair[rows, 64:65])
    row = lax.broadcasted_iota(i32, own_ref.shape, 0)
    lane = lax.broadcasted_iota(i32, own_ref.shape, 1)
    adapter = jnp.concatenate([adapter_ref[...].reshape(1, 32)] * 4, axis=1).astype(f32)
    adapter = jnp.sum(jnp.where(lane == row, adapter, 0.0), axis=1, keepdims=True)
    own_ref[...] = jnp.broadcast_to(adapter, own_ref.shape).astype(i32)


def project(att_ref, adapter_ref, weight_ref, down_ref, up_ref, out_ref, rows_ref):
    projected = jnp.zeros((32, 256), f32)
    reduced = jnp.zeros((32, down_ref.shape[1]), f32)
    for part, head in enumerate((0, 2, 1, 3)):
        rows = slice(128 * head, 128 * head + 128)
        projected = projected + jnp.dot(
            att_ref[part], weight_ref[rows, :], preferred_element_type=f32
        )
        reduced = reduced + jnp.dot(att_ref[part], down_ref[rows, :], preferred_element_type=f32)
    column = lax.broadcasted_iota(i32, reduced.shape, 1)
    chosen = jnp.where(column // RANK == adapter_ref[:, 0:1], reduced, 0.0)
    upper = chosen.astype(bf16)
    lower = (chosen - upper.astype(f32)).astype(bf16)
    both = jnp.dot(
        jnp.concatenate([upper, lower], axis=0), up_ref[...], preferred_element_type=f32
    )
    result = projected + ADAPTER_SCALE * (both[:32] + both[32:])
    for j in range(16):
        rows_ref[j, 0:2, :] = result[2 * j : 2 * j + 2, :128]
        rows_ref[j, 2:4, :] = result[2 * j : 2 * j + 2, 128:]
    out_ref[...] = rows_ref[...].astype(bf16)


def finish(x_ref, out_ref):
    result = jnp.sum(x_ref[...].astype(f32), axis=0)
    out_ref[:, 0:128] = result[0:2].astype(out_ref.dtype)
    out_ref[:, 128:256] = result[2:4].astype(out_ref.dtype)


def on_device(
    queries,
    key_value_pages,
    request_page_index,
    lengths,
    request_adapter_index,
    output_weight,
    down_weight_columns,
    up_weight_rows,
):
    shape = jax.ShapeDtypeStruct
    pages_here, slice_tokens, kv_heads, row = key_value_pages.shape
    page_size = slice_tokens * lax.axis_size(MP)
    scale = 1.0 / math.sqrt(row // 2)

    with jax.named_scope("queries_over_kv"):
        packed = call(
            pack_queries,
            shape((32, 4, 128), bf16),
            queries.T,
            cost=pl.CostEstimate(flops=10**10, bytes_accessed=10**7, transcendentals=0),
        )
        spread = exchange(packed, KV, QUERY_FIRST)
    with jax.named_scope("pages_over_y"):
        tokens = pages_here * slice_tokens
        pieces = call(
            sort_pages,
            (shape((2, 2, tokens, row // 2), bf16),) * 4,
            key_value_pages,
            scratch=[pltpu.VMEM((2, tokens // 4 * kv_heads, row // 2), f32)],
        )
        pieces = list(pieces)
        for step in range(1, 4):
            ring = [(k, (k + step) % 4) for k in range(4)]
            pieces[step] = lax.ppermute(pieces[step], "y", ring)
    with jax.named_scope("queries_over_mp"):
        regrouped = call(
            regroup_queries,
            shape((16, 2, 16, 128), bf16),
            spread,
            cost=pl.CostEstimate(flops=10**11, bytes_accessed=10**8, transcendentals=0),
        )
        own_queries = exchange(regrouped, MP)
    with jax.named_scope("attention"):
        partial, adapter = call(
            lambda *refs: attend(scale, page_size, *refs),
            (shape((16, 40, 128), bf16), shape((32, 128), i32)),
            own_queries,
            *pieces,
            request_page_index,
            lengths,
            request_adapter_index,
            scratch=[pltpu.VMEM((4, 256, 256), f32)],
        )
    with jax.named_scope("merge"):
        near = call(merge_near, shape((8, 40, 128), bf16), exchange(partial, SPLIT))
        attended = call(merge_far, shape((4, 32, 128), bf16), exchange(near, FAR, MERGE_FIRST))
        attended = exchange(attended, NEAR)
    with jax.named_scope("projection"):
        result = call(
            project,
            shape((16, 4, 128), bf16),
            attended,
            adapter,
            output_weight,
            down_weight_columns,
            up_weight_rows,
            scratch=[pltpu.VMEM((16, 4, 128), f32)],
        )
        return call(finish, shape((2, 256), bf16), exchange(result, MP))


def solution(mesh):
    fine = Mesh(mesh.devices.reshape(8, 2, 2, 4, 4), KV + MP)
    in_specs = (
        P(None, KV + MP),
        P(KV, MP, None, None),
        P(),
        P(),
        P(),
        P(MP, KV),
        P(MP, None),
        P(None, KV),
    )
    return jax.shard_map(
        on_device, mesh=fine, in_specs=in_specs, out_specs=P(MP, KV), check_vma=False
    )
```

```python
import math

import jax
import jax.numpy as jnp
from jax import lax
from jax.experimental import pallas as pl
from jax.experimental.pallas import tpu as pltpu
from jax.sharding import Mesh
from jax.sharding import PartitionSpec as P

RANK = 16
LOW = -1e30
FLOOR = -1e20
ADAPTER_SCALE = 2.0

KV = ("zo", "zn", "c")
MP = ("y", "x")
NEAR = ("zn", "c")
SPLIT = ("zn", "c", "x")
FAR = ("zo",)

bf16 = jnp.bfloat16
f32 = jnp.float32
i32 = jnp.int32


QUERY_FIRST = 24
MERGE_FIRST = 3


def exchange(value, axes, first=0):
    members = value.shape[0]
    groups = [[(first + k) % members for k in range(members)]] if first else None
    return lax.all_to_all(
        value, axes, split_axis=0, concat_axis=0, tiled=True, axis_index_groups=groups
    )


def call(kernel, out_shape, *operands, scratch=(), cost=None):
    return pl.pallas_call(
        kernel,
        out_shape=out_shape,
        in_specs=[pl.BlockSpec(memory_space=pltpu.VMEM)] * len(operands),
        out_specs=jax.tree.map(lambda _: pl.BlockSpec(memory_space=pltpu.VMEM), out_shape),
        scratch_shapes=list(scratch),
        cost_estimate=cost,
        compiler_params=pltpu.CompilerParams(vmem_limit_bytes=16 * 1024 * 1024),
    )(*operands)


def pack_queries(q_ref, out_ref):
    q = q_ref[...].astype(f32)
    requests = q.shape[1]
    row = lax.broadcasted_iota(i32, (requests, 128), 0)
    lane = lax.broadcasted_iota(i32, (requests, 128), 1)
    packed = jnp.zeros((4, 128), f32)
    for u in range(4):
        place = (lane == row + u * requests).astype(f32)
        packed = packed + jnp.dot(q[4 * u : 4 * u + 4], place, preferred_element_type=f32)
    out_ref[...] = jnp.broadcast_to(packed.astype(bf16)[None], out_ref.shape)


def sort_pages(kv_ref, *refs):
    *piece_refs, wide_ref = refs
    parts = 4
    pages = kv_ref.shape[0] // parts
    tokens = pages * kv_ref.shape[1]
    y = lax.axis_index("y")
    for k in range(parts):
        wide = kv_ref[pages * k : pages * k + pages].astype(f32).reshape(8 * tokens, 256)
        wide_ref[0] = wide[:, :128]
        wide_ref[1] = wide[:, 128:]
        for step, piece_ref in enumerate(piece_refs):
            for head in range(2):
                first = 2 * lax.rem(y + step, 4) + head
                for side in range(2):
                    rows = wide_ref[side, pl.ds(first, tokens, stride=8), :]
                    to = slice(tokens * k, tokens * k + tokens)
                    piece_ref[head, side, to, :] = rows.astype(bf16)


def count_tokens(page_size, pages, table_ref, length_ref):
    first = lax.axis_index(KV) * pages
    table = jnp.concatenate([table_ref[...]] * 4, axis=0).astype(f32)
    table = jnp.concatenate([table] * 4, axis=1).T[: table_ref.shape[1]].astype(i32)
    length = jnp.concatenate([length_ref[...].reshape(1, 32)] * 4, axis=1)
    start = page_size * lax.broadcasted_iota(i32, table.shape, 0)
    inside = jnp.clip(length - start, 0, page_size).astype(f32)
    rows = [
        jnp.sum(jnp.where(table == first + page, inside, 0.0), axis=0, keepdims=True)
        for page in range(pages)
    ]
    return jnp.concatenate(rows, axis=0).astype(i32)


def regroup_queries(x_ref, out_ref):
    x = x_ref[...].astype(f32)
    x = jnp.concatenate([x[32 - QUERY_FIRST :], x[: 32 - QUERY_FIRST]], axis=0)
    x = x.reshape(8, 4, 4, 128)
    group = lax.broadcasted_iota(i32, (32, 128), 1) // 32
    blocks = [x[:, i].reshape(32, 128) for i in range(4)]
    rows = []
    for u in range(4):
        merged = jnp.zeros((32, 128), f32)
        for i in range(4):
            moved = pltpu.roll(blocks[i], (32 * (i - u)) % 128, 1) if i != u else blocks[i]
            merged = jnp.where(group == i, moved, merged)
        rows.append(merged.reshape(8, 1, 4, 128))
    whole = jnp.concatenate(rows, axis=1).reshape(4, 1, 2, 16, 128).astype(bf16)
    out_ref[...] = jnp.broadcast_to(whole, (4, 4, 2, 16, 128)).reshape(16, 2, 16, 128)


def thirds(value):
    parts = []
    for _ in range(3):
        parts.append(value.astype(bf16).astype(f32))
        value = value - parts[-1]
    return parts


def encode(outputs, peak, total):
    columns = []
    for block in range(4):
        rows = slice(8 * block, 8 * block + 8)
        columns += thirds(peak[rows]) + thirds(total[rows])
    lane = lax.broadcasted_iota(i32, (8, 128), 1)
    tile = jnp.zeros((8, 128), f32)
    for place, column in enumerate(columns):
        tile = jnp.where(lane // 5 == place, column, tile)
    return jnp.concatenate([outputs, tile], axis=0).astype(bf16)


def merged(x_ref):
    x = x_ref[...].astype(f32)
    tile = x[:, 32:40]

    def column(place):
        parts = [
            sum(tile[:, :, 5 * (first + k) : 5 * (first + k) + 1] for k in range(3))
            for first in range(place, 24, 6)
        ]
        return jnp.concatenate(parts, axis=1)

    peaks, totals = column(0), column(3)
    peak = jnp.max(peaks, axis=0)
    factor = jnp.exp(peaks - peak[None])
    outputs = jnp.sum(factor * x[:, 0:32], axis=0)
    return outputs, peak, jnp.sum(factor * totals, axis=0)


def merge_near(x_ref, out_ref):
    out_ref[...] = jnp.broadcast_to(encode(*merged(x_ref))[None], out_ref.shape)


def merge_far(x_ref, out_ref):
    outputs, _, total = merged(x_ref)
    out_ref[...] = (outputs * (1.0 / total)).astype(bf16)


def attend(scale, page_size, q_ref, *refs):
    *pieces, table_ref, length_ref, adapter_ref, out_ref, own_ref, s_ref = refs
    y, x = lax.axis_index("y"), lax.axis_index("x")
    tokens = pieces[0].shape[2]
    pages = tokens // 8
    count = count_tokens(page_size, pages, table_ref, length_ref)
    token = lax.broadcasted_iota(i32, (pages, 8, 128), 1)
    room = (count[:, None, :] - token).reshape(tokens, 128)
    room = jnp.concatenate([room, room], axis=1)
    places = [8 * (4 * lax.rem(y + 4 - step, 4) + x) for step in range(4)]
    for head in range(2):
        queries = q_ref[:, head]
        queries = jnp.concatenate(
            [queries[0:8].reshape(128, 128), queries[8:16].reshape(128, 128)], axis=1
        )
        peak = jnp.full((1, 256), FLOOR, f32)
        for step in range(4):
            scores = jnp.dot(pieces[step][head, 0], queries, preferred_element_type=f32)
            scores = jnp.where(room > places[step], scores * scale, LOW)
            s_ref[step] = scores
            peak = jnp.maximum(peak, jnp.max(scores, axis=0, keepdims=True))
        total = jnp.zeros((1, 256), f32)
        mixed = jnp.zeros((128, 256), f32)
        for step in range(4):
            weights = jnp.exp(s_ref[step] - peak)
            total = total + jnp.sum(weights, axis=0, keepdims=True)
            mixed = mixed + lax.dot_general(
                pieces[step][head, 1],
                weights.astype(bf16),
                (((0,), (0,)), ((), ())),
                preferred_element_type=f32,
            )
        outputs = mixed.T
        row = lax.broadcasted_iota(i32, (128, 256), 0)
        pair = jnp.where(row < 64, peak, total).T
        for bit0 in range(2):
            for half in range(2):
                for bit1 in range(2):
                    start = ((bit0 * 2 + half) * 2 + bit1) * 32
                    rows = slice(start, start + 32)
                    to = (bit0 * 2 + bit1) * 4 + head * 2 + half
                    out_ref[to] = encode(outputs[rows], pair[rows, 0:1], pair[rows, 64:65])
    row = lax.broadcasted_iota(i32, own_ref.shape, 0)
    lane = lax.broadcasted_iota(i32, own_ref.shape, 1)
    adapter = jnp.concatenate([adapter_ref[...].reshape(1, 32)] * 4, axis=1).astype(f32)
    adapter = jnp.sum(jnp.where(lane == row, adapter, 0.0), axis=1, keepdims=True)
    own_ref[...] = jnp.broadcast_to(adapter, own_ref.shape).astype(i32)


def project(att_ref, adapter_ref, weight_ref, down_ref, up_ref, out_ref, rows_ref):
    projected = jnp.zeros((32, 256), f32)
    reduced = jnp.zeros((32, down_ref.shape[1]), f32)
    for part, head in enumerate((0, 2, 1, 3)):
        rows = slice(128 * head, 128 * head + 128)
        projected = projected + jnp.dot(
            att_ref[part], weight_ref[rows, :], preferred_element_type=f32
        )
        reduced = reduced + jnp.dot(att_ref[part], down_ref[rows, :], preferred_element_type=f32)
    column = lax.broadcasted_iota(i32, reduced.shape, 1)
    chosen = jnp.where(column // RANK == adapter_ref[:, 0:1], reduced, 0.0)
    upper = chosen.astype(bf16)
    lower = (chosen - upper.astype(f32)).astype(bf16)
    both = jnp.dot(
        jnp.concatenate([upper, lower], axis=0), up_ref[...], preferred_element_type=f32
    )
    result = projected + ADAPTER_SCALE * (both[:32] + both[32:])
    for j in range(16):
        rows_ref[j, 0:2, :] = result[2 * j : 2 * j + 2, :128]
        rows_ref[j, 2:4, :] = result[2 * j : 2 * j + 2, 128:]
    out_ref[...] = rows_ref[...].astype(bf16)


def finish(x_ref, out_ref):
    result = jnp.sum(x_ref[...].astype(f32), axis=0)
    out_ref[:, 0:128] = result[0:2].astype(out_ref.dtype)
    out_ref[:, 128:256] = result[2:4].astype(out_ref.dtype)


def on_device(
    queries,
    key_value_pages,
    request_page_index,
    lengths,
    request_adapter_index,
    output_weight,
    down_weight_columns,
    up_weight_rows,
):
    shape = jax.ShapeDtypeStruct
    pages_here, slice_tokens, kv_heads, row = key_value_pages.shape
    page_size = slice_tokens * lax.axis_size(MP)
    scale = 1.0 / math.sqrt(row // 2)

    with jax.named_scope("queries_over_kv"):
        packed = call(
            pack_queries,
            shape((32, 4, 128), bf16),
            queries.T,
            cost=pl.CostEstimate(flops=10**10, bytes_accessed=10**7, transcendentals=0),
        )
        spread = exchange(packed, KV, QUERY_FIRST)
    with jax.named_scope("pages_over_y"):
        tokens = pages_here * slice_tokens
        pieces = call(
            sort_pages,
            (shape((2, 2, tokens, row // 2), bf16),) * 4,
            key_value_pages,
            scratch=[pltpu.VMEM((2, tokens // 4 * kv_heads, row // 2), f32)],
        )
        pieces = list(pieces)
        for step in range(1, 4):
            ring = [(k, (k + step) % 4) for k in range(4)]
            pieces[step] = lax.ppermute(pieces[step], "y", ring)
    with jax.named_scope("queries_over_mp"):
        regrouped = call(
            regroup_queries,
            shape((16, 2, 16, 128), bf16),
            spread,
            cost=pl.CostEstimate(flops=10**11, bytes_accessed=10**8, transcendentals=0),
        )
        own_queries = exchange(regrouped, MP)
    with jax.named_scope("attention"):
        partial, adapter = call(
            lambda *refs: attend(scale, page_size, *refs),
            (shape((16, 40, 128), bf16), shape((32, 128), i32)),
            own_queries,
            *pieces,
            request_page_index,
            lengths,
            request_adapter_index,
            scratch=[pltpu.VMEM((4, 256, 256), f32)],
        )
    with jax.named_scope("merge"):
        near = call(merge_near, shape((8, 40, 128), bf16), exchange(partial, SPLIT))
        attended = call(merge_far, shape((32, 128), bf16), exchange(near, FAR, MERGE_FIRST))
        attended = lax.all_gather(attended, NEAR)
    with jax.named_scope("projection"):
        result = call(
            project,
            shape((16, 4, 128), bf16),
            attended,
            adapter,
            output_weight,
            down_weight_columns,
            up_weight_rows,
            scratch=[pltpu.VMEM((16, 4, 128), f32)],
        )
        return call(finish, shape((2, 256), bf16), exchange(result, MP))


def solution(mesh):
    fine = Mesh(mesh.devices.reshape(8, 2, 2, 4, 4), KV + MP)
    in_specs = (
        P(None, KV + MP),
        P(KV, MP, None, None),
        P(),
        P(),
        P(),
        P(MP, KV),
        P(MP, None),
        P(None, KV),
    )
    return jax.shard_map(
        on_device, mesh=fine, in_specs=in_specs, out_specs=P(MP, KV), check_vma=False
    )
```

```python
import math

import jax
import jax.numpy as jnp
from jax import lax
from jax.experimental import pallas as pl
from jax.experimental.pallas import tpu as pltpu
from jax.sharding import Mesh
from jax.sharding import PartitionSpec as P

RANK = 16
LOW = -1e30
FLOOR = -1e20
ADAPTER_SCALE = 2.0

KV = ("zo", "zn", "c")
MP = ("y", "x")
NEAR = ("zn", "c")
SPLIT = ("zn", "c", "x")
FAR = ("zo",)

bf16 = jnp.bfloat16
f32 = jnp.float32
i32 = jnp.int32


QUERY_FIRST = 24
MERGE_FIRST = 3


def exchange(value, axes, first=0):
    members = value.shape[0]
    groups = [[(first + k) % members for k in range(members)]] if first else None
    return lax.all_to_all(
        value, axes, split_axis=0, concat_axis=0, tiled=True, axis_index_groups=groups
    )


def call(kernel, out_shape, *operands, scratch=(), cost=None):
    return pl.pallas_call(
        kernel,
        out_shape=out_shape,
        in_specs=[pl.BlockSpec(memory_space=pltpu.VMEM)] * len(operands),
        out_specs=jax.tree.map(lambda _: pl.BlockSpec(memory_space=pltpu.VMEM), out_shape),
        scratch_shapes=list(scratch),
        cost_estimate=cost,
        compiler_params=pltpu.CompilerParams(vmem_limit_bytes=16 * 1024 * 1024),
    )(*operands)


def pack_queries(q_ref, out_ref):
    q = q_ref[...].astype(f32)
    requests = q.shape[1]
    row = lax.broadcasted_iota(i32, (requests, 128), 0)
    lane = lax.broadcasted_iota(i32, (requests, 128), 1)
    packed = jnp.zeros((4, 128), f32)
    for u in range(4):
        place = (lane == row + u * requests).astype(f32)
        packed = packed + jnp.dot(q[4 * u : 4 * u + 4], place, preferred_element_type=f32)
    out_ref[...] = jnp.broadcast_to(packed.astype(bf16)[None], out_ref.shape)


def sort_pages(kv_ref, *refs):
    *piece_refs, wide_ref = refs
    parts = 4
    pages = kv_ref.shape[0] // parts
    tokens = pages * kv_ref.shape[1]
    y = lax.axis_index("y")
    for k in range(parts):
        wide = kv_ref[pages * k : pages * k + pages].astype(f32).reshape(8 * tokens, 256)
        wide_ref[0, : 8 * tokens] = wide[:, :128]
        wide_ref[1, : 8 * tokens] = wide[:, 128:]
        for step, piece_ref in enumerate(piece_refs):
            for head in range(2):
                first = 2 * lax.rem(y + step, 4) + head
                for side in range(2):
                    rows = wide_ref[side, pl.ds(first, tokens, stride=8), :]
                    to = slice(tokens * k, tokens * k + tokens)
                    piece_ref[head, side, to, :] = rows.astype(bf16)


def count_tokens(page_size, pages, table_ref, length_ref):
    first = lax.axis_index(KV) * pages
    table = jnp.concatenate([table_ref[...]] * 4, axis=0).astype(f32)
    table = jnp.concatenate([table] * 4, axis=1).T[: table_ref.shape[1]].astype(i32)
    length = jnp.concatenate([length_ref[...].reshape(1, 32)] * 4, axis=1)
    start = page_size * lax.broadcasted_iota(i32, table.shape, 0)
    inside = jnp.clip(length - start, 0, page_size).astype(f32)
    rows = [
        jnp.sum(jnp.where(table == first + page, inside, 0.0), axis=0, keepdims=True)
        for page in range(pages)
    ]
    return jnp.concatenate(rows, axis=0).astype(i32)


def regroup_queries(x_ref, out_ref):
    x = x_ref[...].astype(f32)
    x = jnp.concatenate([x[32 - QUERY_FIRST :], x[: 32 - QUERY_FIRST]], axis=0)
    x = x.reshape(8, 4, 4, 128)
    group = lax.broadcasted_iota(i32, (32, 128), 1) // 32
    blocks = [x[:, i].reshape(32, 128) for i in range(4)]
    rows = []
    for u in range(4):
        merged = jnp.zeros((32, 128), f32)
        for i in range(4):
            moved = pltpu.roll(blocks[i], (32 * (i - u)) % 128, 1) if i != u else blocks[i]
            merged = jnp.where(group == i, moved, merged)
        rows.append(merged.reshape(8, 1, 4, 128))
    whole = jnp.concatenate(rows, axis=1).reshape(4, 1, 2, 16, 128).astype(bf16)
    out_ref[...] = jnp.broadcast_to(whole, (4, 4, 2, 16, 128)).reshape(16, 2, 16, 128)


def thirds(value):
    parts = []
    for _ in range(3):
        parts.append(value.astype(bf16).astype(f32))
        value = value - parts[-1]
    return parts


def encode(outputs, peak, total):
    columns = []
    for block in range(4):
        rows = slice(8 * block, 8 * block + 8)
        columns += thirds(peak[rows]) + thirds(total[rows])
    lane = lax.broadcasted_iota(i32, (8, 128), 1)
    tile = jnp.zeros((8, 128), f32)
    for place, column in enumerate(columns):
        tile = jnp.where(lane // 5 == place, column, tile)
    return jnp.concatenate([outputs, tile], axis=0).astype(bf16)


def merged(x_ref):
    x = x_ref[...].astype(f32)
    tile = x[:, 32:40]

    def column(place):
        parts = [
            sum(tile[:, :, 5 * (first + k) : 5 * (first + k) + 1] for k in range(3))
            for first in range(place, 24, 6)
        ]
        return jnp.concatenate(parts, axis=1)

    peaks, totals = column(0), column(3)
    peak = jnp.max(peaks, axis=0)
    factor = jnp.exp(peaks - peak[None])
    outputs = jnp.sum(factor * x[:, 0:32], axis=0)
    return outputs, peak, jnp.sum(factor * totals, axis=0)


def merge_near(x_ref, out_ref):
    out_ref[...] = jnp.broadcast_to(encode(*merged(x_ref))[None], out_ref.shape)


def merge_far(x_ref, out_ref):
    outputs, _, total = merged(x_ref)
    out_ref[...] = (outputs * (1.0 / total)).astype(bf16)


def attend(scale, page_size, q_ref, *refs):
    *pieces, table_ref, length_ref, adapter_ref, out_ref, own_ref, s_ref = refs
    y, x = lax.axis_index("y"), lax.axis_index("x")
    tokens = pieces[0].shape[2]
    pages = tokens // 8
    count = count_tokens(page_size, pages, table_ref, length_ref)
    token = lax.broadcasted_iota(i32, (pages, 8, 128), 1)
    room = (count[:, None, :] - token).reshape(tokens, 128)
    room = jnp.concatenate([room, room], axis=1)
    places = [8 * (4 * lax.rem(y + 4 - step, 4) + x) for step in range(4)]
    for head in range(2):
        queries = q_ref[:, head]
        queries = jnp.concatenate(
            [queries[0:8].reshape(128, 128), queries[8:16].reshape(128, 128)], axis=1
        )
        peak = jnp.full((1, 256), FLOOR, f32)
        for step in range(4):
            scores = jnp.dot(pieces[step][head, 0], queries, preferred_element_type=f32)
            scores = jnp.where(room > places[step], scores * scale, LOW)
            s_ref[step] = scores
            peak = jnp.maximum(peak, jnp.max(scores, axis=0, keepdims=True))
        total = jnp.zeros((1, 256), f32)
        mixed = jnp.zeros((128, 256), f32)
        for step in range(4):
            weights = jnp.exp(s_ref[step] - peak)
            total = total + jnp.sum(weights, axis=0, keepdims=True)
            mixed = mixed + lax.dot_general(
                pieces[step][head, 1],
                weights.astype(bf16),
                (((0,), (0,)), ((), ())),
                preferred_element_type=f32,
            )
        outputs = mixed.T
        row = lax.broadcasted_iota(i32, (128, 256), 0)
        pair = jnp.where(row < 64, peak, total).T
        for bit0 in range(2):
            for half in range(2):
                for bit1 in range(2):
                    start = ((bit0 * 2 + half) * 2 + bit1) * 32
                    rows = slice(start, start + 32)
                    to = (bit0 * 2 + bit1) * 4 + head * 2 + half
                    out_ref[to] = encode(outputs[rows], pair[rows, 0:1], pair[rows, 64:65])
    row = lax.broadcasted_iota(i32, own_ref.shape, 0)
    lane = lax.broadcasted_iota(i32, own_ref.shape, 1)
    adapter = jnp.concatenate([adapter_ref[...].reshape(1, 32)] * 4, axis=1).astype(f32)
    adapter = jnp.sum(jnp.where(lane == row, adapter, 0.0), axis=1, keepdims=True)
    own_ref[...] = jnp.broadcast_to(adapter, own_ref.shape).astype(i32)


def project(att_ref, adapter_ref, weight_ref, down_ref, up_ref, out_ref, rows_ref):
    projected = jnp.zeros((32, 256), f32)
    reduced = jnp.zeros((32, down_ref.shape[1]), f32)
    for part, head in enumerate((0, 2, 1, 3)):
        rows = slice(128 * head, 128 * head + 128)
        projected = projected + jnp.dot(
            att_ref[part], weight_ref[rows, :], preferred_element_type=f32
        )
        reduced = reduced + jnp.dot(att_ref[part], down_ref[rows, :], preferred_element_type=f32)
    column = lax.broadcasted_iota(i32, reduced.shape, 1)
    chosen = jnp.where(column // RANK == adapter_ref[:, 0:1], reduced, 0.0)
    upper = chosen.astype(bf16)
    lower = (chosen - upper.astype(f32)).astype(bf16)
    both = jnp.dot(
        jnp.concatenate([upper, lower], axis=0), up_ref[...], preferred_element_type=f32
    )
    result = projected + ADAPTER_SCALE * (both[:32] + both[32:])
    for j in range(16):
        rows_ref[j, 0:2, :] = result[2 * j : 2 * j + 2, :128]
        rows_ref[j, 2:4, :] = result[2 * j : 2 * j + 2, 128:]
    out_ref[...] = rows_ref[...].astype(bf16)


def finish(x_ref, out_ref):
    result = jnp.sum(x_ref[...].astype(f32), axis=0)
    out_ref[:, 0:128] = result[0:2].astype(out_ref.dtype)
    out_ref[:, 128:256] = result[2:4].astype(out_ref.dtype)


def on_device(
    queries,
    key_value_pages,
    request_page_index,
    lengths,
    request_adapter_index,
    output_weight,
    down_weight_columns,
    up_weight_rows,
):
    shape = jax.ShapeDtypeStruct
    pages_here, slice_tokens, kv_heads, row = key_value_pages.shape
    page_size = slice_tokens * lax.axis_size(MP)
    scale = 1.0 / math.sqrt(row // 2)

    with jax.named_scope("queries_over_kv"):
        packed = call(
            pack_queries,
            shape((32, 4, 128), bf16),
            queries.T,
            cost=pl.CostEstimate(flops=10**10, bytes_accessed=10**7, transcendentals=0),
        )
        spread = exchange(packed, KV, QUERY_FIRST)
    with jax.named_scope("pages_over_y"):
        tokens = pages_here * slice_tokens
        pieces = call(
            sort_pages,
            (shape((2, 2, tokens, row // 2), bf16),) * 4,
            key_value_pages,
            scratch=[pltpu.VMEM((2, (tokens // 4 + 1) * kv_heads, row // 2), f32)],
        )
        pieces = list(pieces)
        for step in range(1, 4):
            ring = [(k, (k + step) % 4) for k in range(4)]
            pieces[step] = lax.ppermute(pieces[step], "y", ring)
    with jax.named_scope("queries_over_mp"):
        regrouped = call(
            regroup_queries,
            shape((16, 2, 16, 128), bf16),
            spread,
            cost=pl.CostEstimate(flops=10**11, bytes_accessed=10**8, transcendentals=0),
        )
        own_queries = exchange(regrouped, MP)
    with jax.named_scope("attention"):
        partial, adapter = call(
            lambda *refs: attend(scale, page_size, *refs),
            (shape((16, 40, 128), bf16), shape((32, 128), i32)),
            own_queries,
            *pieces,
            request_page_index,
            lengths,
            request_adapter_index,
            scratch=[pltpu.VMEM((4, 256, 256), f32)],
        )
    with jax.named_scope("merge"):
        near = call(merge_near, shape((8, 40, 128), bf16), exchange(partial, SPLIT))
        attended = call(merge_far, shape((32, 128), bf16), exchange(near, FAR, MERGE_FIRST))
        attended = lax.all_gather(attended, NEAR)
    with jax.named_scope("projection"):
        result = call(
            project,
            shape((16, 4, 128), bf16),
            attended,
            adapter,
            output_weight,
            down_weight_columns,
            up_weight_rows,
            scratch=[pltpu.VMEM((16, 4, 128), f32)],
        )
        return call(finish, shape((2, 256), bf16), exchange(result, MP))


def solution(mesh):
    fine = Mesh(mesh.devices.reshape(8, 2, 2, 4, 4), KV + MP)
    in_specs = (
        P(None, KV + MP),
        P(KV, MP, None, None),
        P(),
        P(),
        P(),
        P(MP, KV),
        P(MP, None),
        P(None, KV),
    )
    return jax.shard_map(
        on_device, mesh=fine, in_specs=in_specs, out_specs=P(MP, KV), check_vma=False
    )
```

```python
import math

import jax
import jax.numpy as jnp
from jax import lax
from jax.experimental import pallas as pl
from jax.experimental.pallas import tpu as pltpu
from jax.sharding import Mesh
from jax.sharding import PartitionSpec as P

RANK = 16
LOW = -1e30
FLOOR = -1e20
ADAPTER_SCALE = 2.0

KV = ("zo", "zn", "c")
MP = ("y", "x")
NEAR = ("zn", "c")
SPLIT = ("zn", "c", "x")
FAR = ("zo",)

bf16 = jnp.bfloat16
f32 = jnp.float32
i32 = jnp.int32


QUERY_FIRST = 24
MERGE_FIRST = 3
QUERY_ORDER = sorted(
    range(32), key=lambda k: (k != QUERY_FIRST, abs((k - QUERY_FIRST + 16) % 32 - 16) // 2 * -1, k)
)


def exchange(value, axes, first=0):
    members = value.shape[0]
    groups = [[(first + k) % members for k in range(members)]] if first else None
    return lax.all_to_all(
        value, axes, split_axis=0, concat_axis=0, tiled=True, axis_index_groups=groups
    )


def call(kernel, out_shape, *operands, scratch=(), cost=None):
    return pl.pallas_call(
        kernel,
        out_shape=out_shape,
        in_specs=[pl.BlockSpec(memory_space=pltpu.VMEM)] * len(operands),
        out_specs=jax.tree.map(lambda _: pl.BlockSpec(memory_space=pltpu.VMEM), out_shape),
        scratch_shapes=list(scratch),
        cost_estimate=cost,
        compiler_params=pltpu.CompilerParams(vmem_limit_bytes=16 * 1024 * 1024),
    )(*operands)


def pack_queries(q_ref, out_ref):
    q = q_ref[...].astype(f32)
    requests = q.shape[1]
    row = lax.broadcasted_iota(i32, (requests, 128), 0)
    lane = lax.broadcasted_iota(i32, (requests, 128), 1)
    packed = jnp.zeros((4, 128), f32)
    for u in range(4):
        place = (lane == row + u * requests).astype(f32)
        packed = packed + jnp.dot(q[4 * u : 4 * u + 4], place, preferred_element_type=f32)
    out_ref[...] = jnp.broadcast_to(packed.astype(bf16)[None], out_ref.shape)


def sort_pages(kv_ref, *refs):
    *piece_refs, wide_ref = refs
    parts = 4
    pages = kv_ref.shape[0] // parts
    tokens = pages * kv_ref.shape[1]
    y = lax.axis_index("y")
    for k in range(parts):
        wide = kv_ref[pages * k : pages * k + pages].astype(f32).reshape(8 * tokens, 256)
        wide_ref[0, : 8 * tokens] = wide[:, :128]
        wide_ref[1, : 8 * tokens] = wide[:, 128:]
        for step, piece_ref in enumerate(piece_refs):
            for head in range(2):
                first = 2 * lax.rem(y + step, 4) + head
                for side in range(2):
                    rows = wide_ref[side, pl.ds(first, tokens, stride=8), :]
                    to = slice(tokens * k, tokens * k + tokens)
                    piece_ref[head, side, to, :] = rows.astype(bf16)


def count_tokens(page_size, pages, table_ref, length_ref):
    first = lax.axis_index(KV) * pages
    table = jnp.concatenate([table_ref[...]] * 4, axis=0).astype(f32)
    table = jnp.concatenate([table] * 4, axis=1).T[: table_ref.shape[1]].astype(i32)
    length = jnp.concatenate([length_ref[...].reshape(1, 32)] * 4, axis=1)
    start = page_size * lax.broadcasted_iota(i32, table.shape, 0)
    inside = jnp.clip(length - start, 0, page_size).astype(f32)
    rows = [
        jnp.sum(jnp.where(table == first + page, inside, 0.0), axis=0, keepdims=True)
        for page in range(pages)
    ]
    return jnp.concatenate(rows, axis=0).astype(i32)


def regroup_queries(x_ref, out_ref):
    x = x_ref[...].astype(f32)
    places = [QUERY_ORDER.index(k) for k in range(32)]
    x = jnp.concatenate([x[place : place + 1] for place in places], axis=0)
    x = x.reshape(8, 4, 4, 128)
    group = lax.broadcasted_iota(i32, (32, 128), 1) // 32
    blocks = [x[:, i].reshape(32, 128) for i in range(4)]
    rows = []
    for u in range(4):
        merged = jnp.zeros((32, 128), f32)
        for i in range(4):
            moved = pltpu.roll(blocks[i], (32 * (i - u)) % 128, 1) if i != u else blocks[i]
            merged = jnp.where(group == i, moved, merged)
        rows.append(merged.reshape(8, 1, 4, 128))
    whole = jnp.concatenate(rows, axis=1).reshape(4, 1, 2, 16, 128).astype(bf16)
    out_ref[...] = jnp.broadcast_to(whole, (4, 4, 2, 16, 128)).reshape(16, 2, 16, 128)


def thirds(value):
    parts = []
    for _ in range(3):
        parts.append(value.astype(bf16).astype(f32))
        value = value - parts[-1]
    return parts


def encode(outputs, peak, total):
    columns = []
    for block in range(4):
        rows = slice(8 * block, 8 * block + 8)
        columns += thirds(peak[rows]) + thirds(total[rows])
    lane = lax.broadcasted_iota(i32, (8, 128), 1)
    tile = jnp.zeros((8, 128), f32)
    for place, column in enumerate(columns):
        tile = jnp.where(lane // 5 == place, column, tile)
    return jnp.concatenate([outputs, tile], axis=0).astype(bf16)


def merged(x_ref):
    x = x_ref[...].astype(f32)
    tile = x[:, 32:40]

    def column(place):
        parts = [
            sum(tile[:, :, 5 * (first + k) : 5 * (first + k) + 1] for k in range(3))
            for first in range(place, 24, 6)
        ]
        return jnp.concatenate(parts, axis=1)

    peaks, totals = column(0), column(3)
    peak = jnp.max(peaks, axis=0)
    factor = jnp.exp(peaks - peak[None])
    outputs = jnp.sum(factor * x[:, 0:32], axis=0)
    return outputs, peak, jnp.sum(factor * totals, axis=0)


def merge_near(x_ref, out_ref):
    out_ref[...] = jnp.broadcast_to(encode(*merged(x_ref))[None], out_ref.shape)


def merge_far(x_ref, out_ref):
    outputs, _, total = merged(x_ref)
    out_ref[...] = (outputs * (1.0 / total)).astype(bf16)


def attend(scale, page_size, q_ref, *refs):
    *pieces, table_ref, length_ref, adapter_ref, out_ref, own_ref, s_ref = refs
    y, x = lax.axis_index("y"), lax.axis_index("x")
    tokens = pieces[0].shape[2]
    pages = tokens // 8
    count = count_tokens(page_size, pages, table_ref, length_ref)
    token = lax.broadcasted_iota(i32, (pages, 8, 128), 1)
    room = (count[:, None, :] - token).reshape(tokens, 128)
    room = jnp.concatenate([room, room], axis=1)
    places = [8 * (4 * lax.rem(y + 4 - step, 4) + x) for step in range(4)]
    for head in range(2):
        queries = q_ref[:, head]
        queries = jnp.concatenate(
            [queries[0:8].reshape(128, 128), queries[8:16].reshape(128, 128)], axis=1
        )
        peak = jnp.full((1, 256), FLOOR, f32)
        for step in range(4):
            scores = jnp.dot(pieces[step][head, 0], queries, preferred_element_type=f32)
            scores = jnp.where(room > places[step], scores * scale, LOW)
            s_ref[step] = scores
            peak = jnp.maximum(peak, jnp.max(scores, axis=0, keepdims=True))
        total = jnp.zeros((1, 256), f32)
        mixed = jnp.zeros((128, 256), f32)
        for step in range(4):
            weights = jnp.exp(s_ref[step] - peak)
            total = total + jnp.sum(weights, axis=0, keepdims=True)
            mixed = mixed + lax.dot_general(
                pieces[step][head, 1],
                weights.astype(bf16),
                (((0,), (0,)), ((), ())),
                preferred_element_type=f32,
            )
        outputs = mixed.T
        row = lax.broadcasted_iota(i32, (128, 256), 0)
        pair = jnp.where(row < 64, peak, total).T
        for bit0 in range(2):
            for half in range(2):
                for bit1 in range(2):
                    start = ((bit0 * 2 + half) * 2 + bit1) * 32
                    rows = slice(start, start + 32)
                    to = (bit0 * 2 + bit1) * 4 + head * 2 + half
                    out_ref[to] = encode(outputs[rows], pair[rows, 0:1], pair[rows, 64:65])
    row = lax.broadcasted_iota(i32, own_ref.shape, 0)
    lane = lax.broadcasted_iota(i32, own_ref.shape, 1)
    adapter = jnp.concatenate([adapter_ref[...].reshape(1, 32)] * 4, axis=1).astype(f32)
    adapter = jnp.sum(jnp.where(lane == row, adapter, 0.0), axis=1, keepdims=True)
    own_ref[...] = jnp.broadcast_to(adapter, own_ref.shape).astype(i32)


def project(att_ref, adapter_ref, weight_ref, down_ref, up_ref, out_ref, rows_ref):
    projected = jnp.zeros((32, 256), f32)
    reduced = jnp.zeros((32, down_ref.shape[1]), f32)
    for part, head in enumerate((0, 2, 1, 3)):
        rows = slice(128 * head, 128 * head + 128)
        projected = projected + jnp.dot(
            att_ref[part], weight_ref[rows, :], preferred_element_type=f32
        )
        reduced = reduced + jnp.dot(att_ref[part], down_ref[rows, :], preferred_element_type=f32)
    column = lax.broadcasted_iota(i32, reduced.shape, 1)
    chosen = jnp.where(column // RANK == adapter_ref[:, 0:1], reduced, 0.0)
    upper = chosen.astype(bf16)
    lower = (chosen - upper.astype(f32)).astype(bf16)
    both = jnp.dot(
        jnp.concatenate([upper, lower], axis=0), up_ref[...], preferred_element_type=f32
    )
    result = projected + ADAPTER_SCALE * (both[:32] + both[32:])
    for j in range(16):
        rows_ref[j, 0:2, :] = result[2 * j : 2 * j + 2, :128]
        rows_ref[j, 2:4, :] = result[2 * j : 2 * j + 2, 128:]
    out_ref[...] = rows_ref[...].astype(bf16)


def finish(x_ref, out_ref):
    result = jnp.sum(x_ref[...].astype(f32), axis=0)
    out_ref[:, 0:128] = result[0:2].astype(out_ref.dtype)
    out_ref[:, 128:256] = result[2:4].astype(out_ref.dtype)


def on_device(
    queries,
    key_value_pages,
    request_page_index,
    lengths,
    request_adapter_index,
    output_weight,
    down_weight_columns,
    up_weight_rows,
):
    shape = jax.ShapeDtypeStruct
    pages_here, slice_tokens, kv_heads, row = key_value_pages.shape
    page_size = slice_tokens * lax.axis_size(MP)
    scale = 1.0 / math.sqrt(row // 2)

    with jax.named_scope("queries_over_kv"):
        packed = call(
            pack_queries,
            shape((32, 4, 128), bf16),
            queries.T,
            cost=pl.CostEstimate(flops=10**10, bytes_accessed=10**7, transcendentals=0),
        )
        spread = lax.all_to_all(
            packed, KV, split_axis=0, concat_axis=0, tiled=True, axis_index_groups=[QUERY_ORDER]
        )
    with jax.named_scope("pages_over_y"):
        tokens = pages_here * slice_tokens
        pieces = call(
            sort_pages,
            (shape((2, 2, tokens, row // 2), bf16),) * 4,
            key_value_pages,
            scratch=[pltpu.VMEM((2, (tokens // 4 + 1) * kv_heads, row // 2), f32)],
        )
        pieces = list(pieces)
        for step in range(1, 4):
            ring = [(k, (k + step) % 4) for k in range(4)]
            pieces[step] = lax.ppermute(pieces[step], "y", ring)
    with jax.named_scope("queries_over_mp"):
        regrouped = call(
            regroup_queries,
            shape((16, 2, 16, 128), bf16),
            spread,
            cost=pl.CostEstimate(flops=10**11, bytes_accessed=10**8, transcendentals=0),
        )
        own_queries = exchange(regrouped, MP)
    with jax.named_scope("attention"):
        partial, adapter = call(
            lambda *refs: attend(scale, page_size, *refs),
            (shape((16, 40, 128), bf16), shape((32, 128), i32)),
            own_queries,
            *pieces,
            request_page_index,
            lengths,
            request_adapter_index,
            scratch=[pltpu.VMEM((4, 256, 256), f32)],
        )
    with jax.named_scope("merge"):
        near = call(merge_near, shape((8, 40, 128), bf16), exchange(partial, SPLIT))
        attended = call(merge_far, shape((32, 128), bf16), exchange(near, FAR, MERGE_FIRST))
        attended = lax.all_gather(attended, NEAR)
    with jax.named_scope("projection"):
        result = call(
            project,
            shape((16, 4, 128), bf16),
            attended,
            adapter,
            output_weight,
            down_weight_columns,
            up_weight_rows,
            scratch=[pltpu.VMEM((16, 4, 128), f32)],
        )
        return call(finish, shape((2, 256), bf16), exchange(result, MP))


def solution(mesh):
    fine = Mesh(mesh.devices.reshape(8, 2, 2, 4, 4), KV + MP)
    in_specs = (
        P(None, KV + MP),
        P(KV, MP, None, None),
        P(),
        P(),
        P(),
        P(MP, KV),
        P(MP, None),
        P(None, KV),
    )
    return jax.shard_map(
        on_device, mesh=fine, in_specs=in_specs, out_specs=P(MP, KV), check_vma=False
    )
```

```python
import math

import jax
import jax.numpy as jnp
from jax import lax
from jax.experimental import pallas as pl
from jax.experimental.pallas import tpu as pltpu
from jax.sharding import Mesh
from jax.sharding import PartitionSpec as P

RANK = 16
LOW = -1e30
FLOOR = -1e20
ADAPTER_SCALE = 2.0

KV = ("zo", "zn", "c")
MP = ("y", "x")
NEAR = ("zn", "c")
SPLIT = ("zn", "c", "x")
FAR = ("zo",)

bf16 = jnp.bfloat16
f32 = jnp.float32
i32 = jnp.int32


QUERY_FIRST = 24
MERGE_FIRST = 3
QUERY_ORDER = sorted(
    range(32), key=lambda k: (k != QUERY_FIRST, abs((k - QUERY_FIRST + 16) % 32 - 16) // 2 * -1, k)
)


def exchange(value, axes, first=0):
    members = value.shape[0]
    groups = [[(first + k) % members for k in range(members)]] if first else None
    return lax.all_to_all(
        value, axes, split_axis=0, concat_axis=0, tiled=True, axis_index_groups=groups
    )


def call(kernel, out_shape, *operands, scratch=(), cost=None):
    return pl.pallas_call(
        kernel,
        out_shape=out_shape,
        in_specs=[pl.BlockSpec(memory_space=pltpu.VMEM)] * len(operands),
        out_specs=jax.tree.map(lambda _: pl.BlockSpec(memory_space=pltpu.VMEM), out_shape),
        scratch_shapes=list(scratch),
        cost_estimate=cost,
        compiler_params=pltpu.CompilerParams(vmem_limit_bytes=16 * 1024 * 1024),
    )(*operands)


def pack_queries(q_ref, out_ref):
    q = q_ref[...].astype(f32)
    requests = q.shape[1]
    row = lax.broadcasted_iota(i32, (requests, 128), 0)
    lane = lax.broadcasted_iota(i32, (requests, 128), 1)
    packed = jnp.zeros((4, 128), f32)
    for u in range(4):
        place = (lane == row + u * requests).astype(f32)
        packed = packed + jnp.dot(q[4 * u : 4 * u + 4], place, preferred_element_type=f32)
    out_ref[...] = jnp.broadcast_to(packed.astype(bf16)[None], out_ref.shape)


def sort_pages(kv_ref, *refs):
    *piece_refs, wide_ref = refs
    parts = 4
    pages = kv_ref.shape[0] // parts
    tokens = pages * kv_ref.shape[1]
    y = lax.axis_index("y")
    for k in range(parts):
        wide = kv_ref[pages * k : pages * k + pages].astype(f32).reshape(8 * tokens, 256)
        wide_ref[0, : 8 * tokens] = wide[:, :128]
        wide_ref[1, : 8 * tokens] = wide[:, 128:]
        for step, piece_ref in enumerate(piece_refs):
            for head in range(2):
                first = 2 * lax.rem(y + step, 4) + head
                for side in range(2):
                    rows = wide_ref[side, pl.ds(first, tokens, stride=8), :]
                    to = slice(tokens * k, tokens * k + tokens)
                    piece_ref[head, side, to, :] = rows.astype(bf16)


def count_tokens(page_size, pages, table_ref, length_ref):
    first = lax.axis_index(KV) * pages
    table = jnp.concatenate([table_ref[...]] * 4, axis=0).astype(f32)
    table = jnp.concatenate([table] * 4, axis=1).T[: table_ref.shape[1]].astype(i32)
    length = jnp.concatenate([length_ref[...].reshape(1, 32)] * 4, axis=1)
    start = page_size * lax.broadcasted_iota(i32, table.shape, 0)
    inside = jnp.clip(length - start, 0, page_size)
    page = first + lax.broadcasted_iota(i32, (pages, 128), 0)
    count = jnp.zeros((pages, 128), i32)
    for slot in range(table.shape[0]):
        found = table[slot : slot + 1] == page
        count = count + jnp.where(found, inside[slot : slot + 1], 0)
    return count


def regroup_queries(x_ref, out_ref):
    x = x_ref[...].astype(f32)
    places = [QUERY_ORDER.index(k) for k in range(32)]
    x = jnp.concatenate([x[place : place + 1] for place in places], axis=0)
    x = x.reshape(8, 4, 4, 128)
    group = lax.broadcasted_iota(i32, (32, 128), 1) // 32
    blocks = [x[:, i].reshape(32, 128) for i in range(4)]
    rows = []
    for u in range(4):
        merged = jnp.zeros((32, 128), f32)
        for i in range(4):
            moved = pltpu.roll(blocks[i], (32 * (i - u)) % 128, 1) if i != u else blocks[i]
            merged = jnp.where(group == i, moved, merged)
        rows.append(merged.reshape(8, 1, 4, 128))
    whole = jnp.concatenate(rows, axis=1).reshape(4, 1, 2, 16, 128).astype(bf16)
    out_ref[...] = jnp.broadcast_to(whole, (4, 4, 2, 16, 128)).reshape(16, 2, 16, 128)


def thirds(value):
    parts = []
    for _ in range(3):
        parts.append(value.astype(bf16).astype(f32))
        value = value - parts[-1]
    return parts


def encode(outputs, peak, total):
    columns = []
    for block in range(4):
        rows = slice(8 * block, 8 * block + 8)
        columns += thirds(peak[rows]) + thirds(total[rows])
    lane = lax.broadcasted_iota(i32, (8, 128), 1)
    tile = jnp.zeros((8, 128), f32)
    for place, column in enumerate(columns):
        tile = jnp.where(lane // 5 == place, column, tile)
    return jnp.concatenate([outputs, tile], axis=0).astype(bf16)


def merged(x_ref):
    x = x_ref[...].astype(f32)
    tile = x[:, 32:40]

    members = tile.shape[0]
    tile = tile.reshape(8 * members, 128)
    tile = tile + pltpu.roll(tile, 123, 1) + pltpu.roll(tile, 118, 1)
    tile = tile.reshape(members, 8, 128)
    parts = []
    for block in range(4):
        lane = 30 * block
        peaks = tile[:, :, lane : lane + 1]
        peak = jnp.max(peaks, axis=0)
        factor = jnp.exp(peaks - peak[None])
        outputs = jnp.sum(factor * x[:, 8 * block : 8 * block + 8], axis=0)
        parts.append((outputs, peak, jnp.sum(factor * tile[:, :, lane + 15 : lane + 16], axis=0)))
    return tuple(jnp.concatenate(part, axis=0) for part in zip(*parts))


def merge_near(x_ref, out_ref):
    out_ref[...] = jnp.broadcast_to(encode(*merged(x_ref))[None], out_ref.shape)


def merge_far(x_ref, out_ref):
    outputs, _, total = merged(x_ref)
    out_ref[...] = (outputs * (1.0 / total)).astype(bf16)


def attend(scale, page_size, q_ref, *refs):
    *pieces, table_ref, length_ref, adapter_ref, out_ref, own_ref, s_ref = refs
    y, x = lax.axis_index("y"), lax.axis_index("x")
    tokens = pieces[0].shape[2]
    pages = tokens // 8
    count = count_tokens(page_size, pages, table_ref, length_ref)
    token = lax.broadcasted_iota(i32, (pages, 8, 128), 1)
    room = (count[:, None, :] - token).reshape(tokens, 128)
    room = jnp.concatenate([room, room], axis=1)
    places = [8 * (4 * lax.rem(y + 4 - step, 4) + x) for step in range(4)]
    for head in range(2):
        queries = q_ref[:, head]
        queries = jnp.concatenate(
            [queries[0:8].reshape(128, 128), queries[8:16].reshape(128, 128)], axis=1
        )
        peak = jnp.full((1, 256), FLOOR, f32)
        for step in range(4):
            scores = jnp.dot(pieces[step][head, 0], queries, preferred_element_type=f32)
            scores = jnp.where(room > places[step], scores * scale, LOW)
            s_ref[step] = scores
            peak = jnp.maximum(peak, jnp.max(scores, axis=0, keepdims=True))
        total = jnp.zeros((1, 256), f32)
        mixed = jnp.zeros((128, 256), f32)
        for step in range(4):
            weights = jnp.exp(s_ref[step] - peak)
            total = total + jnp.sum(weights, axis=0, keepdims=True)
            mixed = mixed + lax.dot_general(
                pieces[step][head, 1],
                weights.astype(bf16),
                (((0,), (0,)), ((), ())),
                preferred_element_type=f32,
            )
        outputs = mixed.T
        row = lax.broadcasted_iota(i32, (128, 256), 0)
        pair = jnp.where(row < 64, peak, total).T
        for bit0 in range(2):
            for half in range(2):
                for bit1 in range(2):
                    start = ((bit0 * 2 + half) * 2 + bit1) * 32
                    rows = slice(start, start + 32)
                    to = (bit0 * 2 + bit1) * 4 + head * 2 + half
                    out_ref[to] = encode(outputs[rows], pair[rows, 0:1], pair[rows, 64:65])
    row = lax.broadcasted_iota(i32, own_ref.shape, 0)
    lane = lax.broadcasted_iota(i32, own_ref.shape, 1)
    adapter = jnp.concatenate([adapter_ref[...].reshape(1, 32)] * 4, axis=1).astype(f32)
    adapter = jnp.sum(jnp.where(lane == row, adapter, 0.0), axis=1, keepdims=True)
    own_ref[...] = jnp.broadcast_to(adapter, own_ref.shape).astype(i32)


def project(att_ref, adapter_ref, weight_ref, down_ref, up_ref, out_ref, rows_ref):
    projected = jnp.zeros((32, 256), f32)
    reduced = jnp.zeros((32, down_ref.shape[1]), f32)
    for part, head in enumerate((0, 2, 1, 3)):
        rows = slice(128 * head, 128 * head + 128)
        projected = projected + jnp.dot(
            att_ref[part], weight_ref[rows, :], preferred_element_type=f32
        )
        reduced = reduced + jnp.dot(att_ref[part], down_ref[rows, :], preferred_element_type=f32)
    column = lax.broadcasted_iota(i32, reduced.shape, 1)
    chosen = jnp.where(column // RANK == adapter_ref[:, 0:1], reduced, 0.0)
    upper = chosen.astype(bf16)
    lower = (chosen - upper.astype(f32)).astype(bf16)
    both = jnp.dot(
        jnp.concatenate([upper, lower], axis=0), up_ref[...], preferred_element_type=f32
    )
    result = projected + ADAPTER_SCALE * (both[:32] + both[32:])
    for j in range(16):
        rows_ref[j, 0:2, :] = result[2 * j : 2 * j + 2, :128]
        rows_ref[j, 2:4, :] = result[2 * j : 2 * j + 2, 128:]
    out_ref[...] = rows_ref[...].astype(bf16)


def finish(x_ref, out_ref):
    result = jnp.sum(x_ref[...].astype(f32), axis=0)
    out_ref[:, 0:128] = result[0:2].astype(out_ref.dtype)
    out_ref[:, 128:256] = result[2:4].astype(out_ref.dtype)


def on_device(
    queries,
    key_value_pages,
    request_page_index,
    lengths,
    request_adapter_index,
    output_weight,
    down_weight_columns,
    up_weight_rows,
):
    shape = jax.ShapeDtypeStruct
    pages_here, slice_tokens, kv_heads, row = key_value_pages.shape
    page_size = slice_tokens * lax.axis_size(MP)
    scale = 1.0 / math.sqrt(row // 2)

    with jax.named_scope("queries_over_kv"):
        packed = call(
            pack_queries,
            shape((32, 4, 128), bf16),
            queries.T,
            cost=pl.CostEstimate(flops=10**10, bytes_accessed=10**7, transcendentals=0),
        )
        spread = lax.all_to_all(
            packed, KV, split_axis=0, concat_axis=0, tiled=True, axis_index_groups=[QUERY_ORDER]
        )
    with jax.named_scope("pages_over_y"):
        tokens = pages_here * slice_tokens
        pieces = call(
            sort_pages,
            (shape((2, 2, tokens, row // 2), bf16),) * 4,
            key_value_pages,
            scratch=[pltpu.VMEM((2, (tokens // 4 + 1) * kv_heads, row // 2), f32)],
        )
        pieces = list(pieces)
        for step in range(1, 4):
            ring = [(k, (k + step) % 4) for k in range(4)]
            pieces[step] = lax.ppermute(pieces[step], "y", ring)
    with jax.named_scope("queries_over_mp"):
        regrouped = call(
            regroup_queries,
            shape((16, 2, 16, 128), bf16),
            spread,
            cost=pl.CostEstimate(flops=10**11, bytes_accessed=10**8, transcendentals=0),
        )
        own_queries = exchange(regrouped, MP)
    with jax.named_scope("attention"):
        partial, adapter = call(
            lambda *refs: attend(scale, page_size, *refs),
            (shape((16, 40, 128), bf16), shape((32, 128), i32)),
            own_queries,
            *pieces,
            request_page_index,
            lengths,
            request_adapter_index,
            scratch=[pltpu.VMEM((4, 256, 256), f32)],
        )
    with jax.named_scope("merge"):
        near = call(merge_near, shape((8, 40, 128), bf16), exchange(partial, SPLIT))
        attended = call(merge_far, shape((32, 128), bf16), exchange(near, FAR, MERGE_FIRST))
        attended = lax.all_gather(attended, NEAR)
    with jax.named_scope("projection"):
        result = call(
            project,
            shape((16, 4, 128), bf16),
            attended,
            adapter,
            output_weight,
            down_weight_columns,
            up_weight_rows,
            scratch=[pltpu.VMEM((16, 4, 128), f32)],
        )
        return call(finish, shape((2, 256), bf16), exchange(result, MP))


def solution(mesh):
    fine = Mesh(mesh.devices.reshape(8, 2, 2, 4, 4), KV + MP)
    in_specs = (
        P(None, KV + MP),
        P(KV, MP, None, None),
        P(),
        P(),
        P(),
        P(MP, KV),
        P(MP, None),
        P(None, KV),
    )
    return jax.shard_map(
        on_device, mesh=fine, in_specs=in_specs, out_specs=P(MP, KV), check_vma=False
    )
```

```python
import math

import jax
import jax.numpy as jnp
from jax import lax
from jax.experimental import pallas as pl
from jax.experimental.pallas import tpu as pltpu
from jax.sharding import Mesh
from jax.sharding import PartitionSpec as P

RANK = 16
LOW = -1e30
FLOOR = -1e20
ADAPTER_SCALE = 2.0

KV = ("zo", "zn", "c")
MP = ("y", "x")
NEAR = ("zn", "c")
SPLIT = ("zn", "c", "x")
FAR = ("zo",)

bf16 = jnp.bfloat16
f32 = jnp.float32
i32 = jnp.int32


QUERY_FIRST = 25
MERGE_FIRST = 3
QUERY_ORDER = sorted(
    range(32), key=lambda k: (k != QUERY_FIRST, abs((k - QUERY_FIRST + 16) % 32 - 16) // 2 * -1, k)
)


def exchange(value, axes, first=0):
    members = value.shape[0]
    groups = [[(first + k) % members for k in range(members)]] if first else None
    return lax.all_to_all(
        value, axes, split_axis=0, concat_axis=0, tiled=True, axis_index_groups=groups
    )


def call(kernel, out_shape, *operands, scratch=(), cost=None):
    return pl.pallas_call(
        kernel,
        out_shape=out_shape,
        in_specs=[pl.BlockSpec(memory_space=pltpu.VMEM)] * len(operands),
        out_specs=jax.tree.map(lambda _: pl.BlockSpec(memory_space=pltpu.VMEM), out_shape),
        scratch_shapes=list(scratch),
        cost_estimate=cost,
        compiler_params=pltpu.CompilerParams(vmem_limit_bytes=16 * 1024 * 1024),
    )(*operands)


def pack_queries(q_ref, out_ref):
    q = q_ref[...].astype(f32)
    requests = q.shape[1]
    row = lax.broadcasted_iota(i32, (requests, 128), 0)
    lane = lax.broadcasted_iota(i32, (requests, 128), 1)
    packed = jnp.zeros((4, 128), f32)
    for u in range(4):
        place = (lane == row + u * requests).astype(f32)
        packed = packed + jnp.dot(q[4 * u : 4 * u + 4], place, preferred_element_type=f32)
    out_ref[...] = jnp.broadcast_to(packed.astype(bf16)[None], out_ref.shape)


def sort_pages(kv_ref, *refs):
    *piece_refs, wide_ref = refs
    parts = 4
    pages = kv_ref.shape[0] // parts
    tokens = pages * kv_ref.shape[1]
    y = lax.axis_index("y")
    for k in range(parts):
        wide = kv_ref[pages * k : pages * k + pages].astype(f32).reshape(8 * tokens, 256)
        wide_ref[0, : 8 * tokens] = wide[:, :128]
        wide_ref[1, : 8 * tokens] = wide[:, 128:]
        for step, piece_ref in enumerate(piece_refs):
            for head in range(2):
                first = 2 * lax.rem(y + step, 4) + head
                for side in range(2):
                    rows = wide_ref[side, pl.ds(first, tokens, stride=8), :]
                    to = slice(tokens * k, tokens * k + tokens)
                    piece_ref[head, side, to, :] = rows.astype(bf16)


def count_tokens(page_size, pages, table_ref, length_ref):
    first = lax.axis_index(KV) * pages
    table = jnp.concatenate([table_ref[...]] * 4, axis=0).astype(f32)
    table = jnp.concatenate([table] * 4, axis=1).T[: table_ref.shape[1]].astype(i32)
    length = jnp.concatenate([length_ref[...].reshape(1, 32)] * 4, axis=1)
    start = page_size * lax.broadcasted_iota(i32, table.shape, 0)
    inside = jnp.clip(length - start, 0, page_size)
    page = first + lax.broadcasted_iota(i32, (pages, 128), 0)
    count = jnp.zeros((pages, 128), i32)
    for slot in range(table.shape[0]):
        found = table[slot : slot + 1] == page
        count = count + jnp.where(found, inside[slot : slot + 1], 0)
    return count


def regroup_queries(x_ref, out_ref):
    x = x_ref[...].astype(f32)
    places = [QUERY_ORDER.index(k) for k in range(32)]
    x = jnp.concatenate([x[place : place + 1] for place in places], axis=0)
    x = x.reshape(8, 4, 4, 128)
    group = lax.broadcasted_iota(i32, (32, 128), 1) // 32
    blocks = [x[:, i].reshape(32, 128) for i in range(4)]
    rows = []
    for u in range(4):
        merged = jnp.zeros((32, 128), f32)
        for i in range(4):
            moved = pltpu.roll(blocks[i], (32 * (i - u)) % 128, 1) if i != u else blocks[i]
            merged = jnp.where(group == i, moved, merged)
        rows.append(merged.reshape(8, 1, 4, 128))
    whole = jnp.concatenate(rows, axis=1).reshape(4, 1, 2, 16, 128).astype(bf16)
    out_ref[...] = jnp.broadcast_to(whole, (4, 4, 2, 16, 128)).reshape(16, 2, 16, 128)


def thirds(value):
    parts = []
    for _ in range(3):
        parts.append(value.astype(bf16).astype(f32))
        value = value - parts[-1]
    return parts


def encode(outputs, peak, total):
    columns = []
    for block in range(4):
        rows = slice(8 * block, 8 * block + 8)
        columns += thirds(peak[rows]) + thirds(total[rows])
    lane = lax.broadcasted_iota(i32, (8, 128), 1)
    tile = jnp.zeros((8, 128), f32)
    for place, column in enumerate(columns):
        tile = jnp.where(lane // 5 == place, column, tile)
    return jnp.concatenate([outputs, tile], axis=0).astype(bf16)


def merged(x_ref):
    x = x_ref[...].astype(f32)
    tile = x[:, 32:40]

    members = tile.shape[0]
    tile = tile.reshape(8 * members, 128)
    tile = tile + pltpu.roll(tile, 123, 1) + pltpu.roll(tile, 118, 1)
    tile = tile.reshape(members, 8, 128)
    parts = []
    for block in range(4):
        lane = 30 * block
        peaks = tile[:, :, lane : lane + 1]
        peak = jnp.max(peaks, axis=0)
        factor = jnp.exp(peaks - peak[None])
        outputs = jnp.sum(factor * x[:, 8 * block : 8 * block + 8], axis=0)
        parts.append((outputs, peak, jnp.sum(factor * tile[:, :, lane + 15 : lane + 16], axis=0)))
    return tuple(jnp.concatenate(part, axis=0) for part in zip(*parts))


def merge_near(x_ref, out_ref):
    out_ref[...] = jnp.broadcast_to(encode(*merged(x_ref))[None], out_ref.shape)


def merge_far(x_ref, out_ref):
    outputs, _, total = merged(x_ref)
    out_ref[...] = (outputs * (1.0 / total)).astype(bf16)


def attend(scale, page_size, q_ref, *refs):
    *pieces, table_ref, length_ref, adapter_ref, out_ref, own_ref, s_ref = refs
    y, x = lax.axis_index("y"), lax.axis_index("x")
    tokens = pieces[0].shape[2]
    pages = tokens // 8
    count = count_tokens(page_size, pages, table_ref, length_ref)
    token = lax.broadcasted_iota(i32, (pages, 8, 128), 1)
    room = (count[:, None, :] - token).reshape(tokens, 128)
    room = jnp.concatenate([room, room], axis=1)
    places = [8 * (4 * lax.rem(y + 4 - step, 4) + x) for step in range(4)]
    for head in range(2):
        queries = q_ref[:, head]
        queries = jnp.concatenate(
            [queries[0:8].reshape(128, 128), queries[8:16].reshape(128, 128)], axis=1
        )
        peak = jnp.full((1, 256), FLOOR, f32)
        for step in range(4):
            scores = jnp.dot(pieces[step][head, 0], queries, preferred_element_type=f32)
            scores = jnp.where(room > places[step], scores * scale, LOW)
            s_ref[step] = scores
            peak = jnp.maximum(peak, jnp.max(scores, axis=0, keepdims=True))
        total = jnp.zeros((1, 256), f32)
        mixed = jnp.zeros((128, 256), f32)
        for step in range(4):
            weights = jnp.exp(s_ref[step] - peak)
            total = total + jnp.sum(weights, axis=0, keepdims=True)
            mixed = mixed + lax.dot_general(
                pieces[step][head, 1],
                weights.astype(bf16),
                (((0,), (0,)), ((), ())),
                preferred_element_type=f32,
            )
        outputs = mixed.T
        row = lax.broadcasted_iota(i32, (128, 256), 0)
        pair = jnp.where(row < 64, peak, total).T
        for bit0 in range(2):
            for half in range(2):
                for bit1 in range(2):
                    start = ((bit0 * 2 + half) * 2 + bit1) * 32
                    rows = slice(start, start + 32)
                    to = (bit0 * 2 + bit1) * 4 + head * 2 + half
                    out_ref[to] = encode(outputs[rows], pair[rows, 0:1], pair[rows, 64:65])
    row = lax.broadcasted_iota(i32, own_ref.shape, 0)
    lane = lax.broadcasted_iota(i32, own_ref.shape, 1)
    adapter = jnp.concatenate([adapter_ref[...].reshape(1, 32)] * 4, axis=1).astype(f32)
    adapter = jnp.sum(jnp.where(lane == row, adapter, 0.0), axis=1, keepdims=True)
    own_ref[...] = jnp.broadcast_to(adapter, own_ref.shape).astype(i32)


def project(att_ref, adapter_ref, weight_ref, down_ref, up_ref, out_ref, rows_ref):
    projected = jnp.zeros((32, 256), f32)
    reduced = jnp.zeros((32, down_ref.shape[1]), f32)
    for part, head in enumerate((0, 2, 1, 3)):
        rows = slice(128 * head, 128 * head + 128)
        projected = projected + jnp.dot(
            att_ref[part], weight_ref[rows, :], preferred_element_type=f32
        )
        reduced = reduced + jnp.dot(att_ref[part], down_ref[rows, :], preferred_element_type=f32)
    column = lax.broadcasted_iota(i32, reduced.shape, 1)
    chosen = jnp.where(column // RANK == adapter_ref[:, 0:1], reduced, 0.0)
    upper = chosen.astype(bf16)
    lower = (chosen - upper.astype(f32)).astype(bf16)
    both = jnp.dot(
        jnp.concatenate([upper, lower], axis=0), up_ref[...], preferred_element_type=f32
    )
    result = projected + ADAPTER_SCALE * (both[:32] + both[32:])
    for j in range(16):
        rows_ref[j, 0:2, :] = result[2 * j : 2 * j + 2, :128]
        rows_ref[j, 2:4, :] = result[2 * j : 2 * j + 2, 128:]
    out_ref[...] = rows_ref[...].astype(bf16)


def finish(x_ref, out_ref):
    result = jnp.sum(x_ref[...].astype(f32), axis=0)
    out_ref[:, 0:128] = result[0:2].astype(out_ref.dtype)
    out_ref[:, 128:256] = result[2:4].astype(out_ref.dtype)


def on_device(
    queries,
    key_value_pages,
    request_page_index,
    lengths,
    request_adapter_index,
    output_weight,
    down_weight_columns,
    up_weight_rows,
):
    shape = jax.ShapeDtypeStruct
    pages_here, slice_tokens, kv_heads, row = key_value_pages.shape
    page_size = slice_tokens * lax.axis_size(MP)
    scale = 1.0 / math.sqrt(row // 2)

    with jax.named_scope("queries_over_kv"):
        packed = call(
            pack_queries,
            shape((32, 4, 128), bf16),
            queries.T,
            cost=pl.CostEstimate(flops=10**10, bytes_accessed=10**7, transcendentals=0),
        )
        spread = lax.all_to_all(
            packed, KV, split_axis=0, concat_axis=0, tiled=True, axis_index_groups=[QUERY_ORDER]
        )
    with jax.named_scope("pages_over_y"):
        tokens = pages_here * slice_tokens
        pieces = call(
            sort_pages,
            (shape((2, 2, tokens, row // 2), bf16),) * 4,
            key_value_pages,
            scratch=[pltpu.VMEM((2, (tokens // 4 + 1) * kv_heads, row // 2), f32)],
        )
        pieces = list(pieces)
        for step in range(1, 4):
            ring = [(k, (k + step) % 4) for k in range(4)]
            pieces[step] = lax.ppermute(pieces[step], "y", ring)
    with jax.named_scope("queries_over_mp"):
        regrouped = call(
            regroup_queries,
            shape((16, 2, 16, 128), bf16),
            spread,
            cost=pl.CostEstimate(flops=10**11, bytes_accessed=10**8, transcendentals=0),
        )
        own_queries = exchange(regrouped, MP)
    with jax.named_scope("attention"):
        partial, adapter = call(
            lambda *refs: attend(scale, page_size, *refs),
            (shape((16, 40, 128), bf16), shape((32, 128), i32)),
            own_queries,
            *pieces,
            request_page_index,
            lengths,
            request_adapter_index,
            scratch=[pltpu.VMEM((4, 256, 256), f32)],
        )
    with jax.named_scope("merge"):
        near = call(merge_near, shape((8, 40, 128), bf16), exchange(partial, SPLIT))
        attended = call(merge_far, shape((32, 128), bf16), exchange(near, FAR, MERGE_FIRST))
        attended = lax.all_gather(attended, NEAR)
    with jax.named_scope("projection"):
        result = call(
            project,
            shape((16, 4, 128), bf16),
            attended,
            adapter,
            output_weight,
            down_weight_columns,
            up_weight_rows,
            scratch=[pltpu.VMEM((16, 4, 128), f32)],
        )
        return call(finish, shape((2, 256), bf16), exchange(result, MP))


def solution(mesh):
    fine = Mesh(mesh.devices.reshape(8, 2, 2, 4, 4), KV + MP)
    in_specs = (
        P(None, KV + MP),
        P(KV, MP, None, None),
        P(),
        P(),
        P(),
        P(MP, KV),
        P(MP, None),
        P(None, KV),
    )
    return jax.shard_map(
        on_device, mesh=fine, in_specs=in_specs, out_specs=P(MP, KV), check_vma=False
    )
```
